256 devices in a mesh: gx: 16 (over x_lo, y, core), gy: 16 (over x_hi, z).
Axes of the slice: x: 4 (x_hi: 2, x_lo: 2; x = x_hi * 2 + x_lo), y: 4, z: 8, core: 2. Of those that a mesh axis runs over, the one named last changes fastest.
Arguments:
- velocity: float32 [3, 256, 128, 128], P(None, 'gx', 'gy'), may hold values from -24 to 24
- viscosity: float32 [256, 128, 128], P('gx', 'gy'), may hold values from 25 to 400
Outputs:
- half_step: float32 [3, 256, 128, 128], P(None, 'gx', 'gy')
- advanced: float32 [3, 256, 128, 128], P(None, 'gx', 'gy')
The draws below stay inside these ranges and needn't reach their ends.
All inputs are finite; a program needn't handle non-finite values.
Results may differ from the reference program's by a relative error of at most 0.0003.
Values sent between devices are 32-bit elements; how exact they have to be, the bound alone decides.
A program may use at most 64 MiB of HBM per device.

```python
import math
import jax
import jax.numpy as jnp
from jax import lax

Z = 128
NX = 256
NY = 128


def draw_velocity(key, part):
    dimensions = (3, NX, NY, Z)
    fluctuation = jax.random.truncated_normal(key, -4.0, 4.0, dimensions, jnp.float32)
    return fluctuation * 6.0


def shard_levels(key, shape, split, smallest, top_value):
    factor_of = 1.0
    for position, shards_of in split:
        steps = jax.random.uniform(jax.random.fold_in(jax.random.fold_in(key, 6), position), (shards_of,), jnp.float32, smallest / len(split), top_value / len(split))
        factor_of = factor_of * jnp.repeat(jnp.exp(steps), shape[position] // shards_of).reshape((-1,) + (1,) * (len(shape) - 1 - position))
    return factor_of


def setup_inputs(seed: int = 0) -> dict:
    key_of = jax.random.split(jax.random.key(seed), 3)
    return {
        "velocity": draw_velocity(jax.random.fold_in(key_of[2], 71), 0),
        "viscosity": jnp.clip(jnp.exp(math.log(400.0) - 2.7725887 * jax.random.uniform(key_of[1], (NX, NY, Z), jnp.float32) ** shard_levels(key_of[1], (NX, NY, Z), ((0, 16), (1, 16)), -0.2, 0.2)), 25.0, 400.0),
    }


def identity_block(system_size, batch_rank):
    return jnp.eye(system_size, dtype=jnp.float32).reshape((1, system_size, system_size) + (1,) * batch_rank)


def small_product(factor_one, factor_two):
    inner_size = factor_one.shape[2]
    total = factor_one[:, :, 0, None] * factor_two[:, None, 0]
    for inner_at in range(1, inner_size):
        total = total + factor_one[:, :, inner_at, None] * factor_two[:, None, inner_at]
    return total


def small_inverse(matrix):
    system_size = matrix.shape[1]
    matrix_rows = [[matrix[:, row_at, col_at] for col_at in range(system_size)] for row_at in range(system_size)]
    ones_part = jnp.ones_like(matrix_rows[0][0])
    zero_part = jnp.zeros_like(matrix_rows[0][0])
    inverse_rows = [[ones_part if row_at == col_at else zero_part for col_at in range(system_size)] for row_at in range(system_size)]
    for pivot_at in range(system_size):
        scaling = 1.0 / matrix_rows[pivot_at][pivot_at]
        matrix_rows[pivot_at] = [element * scaling for element in matrix_rows[pivot_at]]
        inverse_rows[pivot_at] = [element * scaling for element in inverse_rows[pivot_at]]
        for row_at in range(system_size):
            if row_at != pivot_at:
                factor = matrix_rows[row_at][pivot_at]
                matrix_rows[row_at] = [matrix_rows[row_at][col_at] - factor * matrix_rows[pivot_at][col_at] for col_at in range(system_size)]
                inverse_rows[row_at] = [inverse_rows[row_at][col_at] - factor * inverse_rows[pivot_at][col_at] for col_at in range(system_size)]
    return jnp.stack([jnp.stack(inverse_rows[row_at], axis=1) for row_at in range(system_size)], axis=1)


def cyclic_reduce(band_low, diagonal, band_high, source, fetcher, periodic, extent):
    stride = 1
    while stride < extent:
        behind, onward = fetcher((band_low, diagonal, band_high, source), stride)
        weight_behind = -small_product(band_low, small_inverse(behind[1]))
        weight_onward = -small_product(band_high, small_inverse(onward[1]))
        next_low = small_product(weight_behind, behind[0])
        next_high = small_product(weight_onward, onward[2])
        diagonal = diagonal + small_product(weight_behind, behind[2]) + small_product(weight_onward, onward[0])
        source = source + small_product(weight_behind, behind[3]) + small_product(weight_onward, onward[3])
        band_low, band_high = next_low, next_high
        stride = stride * 2
    if periodic:
        diagonal = diagonal + band_low + band_high
    return small_product(small_inverse(diagonal), source)


def rolled_fetch(members, stride):
    behind = tuple(jnp.roll(member, stride, axis=0) for member in members)
    onward = tuple(jnp.roll(member, -stride, axis=0) for member in members)
    return behind, onward


def walled_fetch(members, stride):
    identity = identity_block(members[1].shape[1], members[1].ndim - 3)
    fillers = [jnp.zeros_like(member) for member in members]
    fillers[1] = jnp.broadcast_to(identity, members[1].shape)
    behind = tuple(jnp.concatenate([filler[:stride], member[:-stride]], axis=0) for filler, member in zip(fillers, members))
    onward = tuple(jnp.concatenate([member[stride:], filler[:stride]], axis=0) for filler, member in zip(fillers, members))
    return behind, onward


def pair_block(top_left, top_right, bottom_left, bottom_right):
    return jnp.stack([jnp.stack([top_left, top_right], axis=1), jnp.stack([bottom_left, bottom_right], axis=1)], axis=1)


def line_blocks_x(padded):
    cell_count = padded.shape[0] - 4
    first = (padded[1:cell_count + 2] + padded[2:cell_count + 3]) * 0.5
    second = (padded[0:cell_count + 2] + padded[2:cell_count + 4]) * 0.125
    first_here = first[1:cell_count + 1]
    first_back = first[0:cell_count]
    second_here = second[2:cell_count + 2]
    second_back = second[0:cell_count]
    cell_diag = 1.0 + first_here + first_back + second_here + second_back
    zero_part = jnp.zeros_like(cell_diag[0::2])
    diagonal = pair_block(cell_diag[0::2], -first_here[0::2], -first_here[0::2], cell_diag[1::2])
    band_high = pair_block(-second_here[0::2], zero_part, -first_here[1::2], -second_here[1::2])
    band_low = pair_block(-second_back[0::2], -first_back[0::2], zero_part, -second_back[1::2])
    return band_low, diagonal, band_high


def line_blocks_y(padded):
    cell_count = padded.shape[0] - 2
    face = padded[0:cell_count + 1] + padded[1:cell_count + 2]
    diagonal = (1.0 + face[1:] + face[:-1])[:, None, None]
    band_high = (-face[1:])[:, None, None]
    band_low = (-face[:-1])[:, None, None]
    return band_low, diagonal, band_high


def solve_stream_lines(field, coefficient):
    padded = jnp.concatenate([coefficient[-2:], coefficient, coefficient[:2]], axis=0)
    band_low, diagonal, band_high = line_blocks_x(padded)
    block_count = field.shape[1] // 2
    source = field.reshape(3, block_count, 2, field.shape[2], field.shape[3]).transpose(1, 2, 0, 3, 4)
    solved = cyclic_reduce(band_low, diagonal, band_high, source, rolled_fetch, True, block_count)
    return solved.transpose(2, 0, 1, 3, 4).reshape(field.shape)


def solve_normal_lines(field, coefficient):
    padded = jnp.pad(coefficient.transpose(1, 0, 2), ((1, 1), (0, 0), (0, 0)))
    band_low, diagonal, band_high = line_blocks_y(padded)
    source = field.transpose(2, 0, 1, 3)[:, None]
    solved = cyclic_reduce(band_low, diagonal, band_high, source, walled_fetch, False, field.shape[2])
    return solved[:, 0].transpose(1, 2, 0, 3)


def reference(velocity, viscosity):
    plane_group = 2
    group_count = Z // plane_group
    grouped_velocity = velocity.reshape(3, NX, NY, group_count, plane_group).transpose(3, 0, 1, 2, 4)
    grouped_viscosity = viscosity.reshape(NX, NY, group_count, plane_group).transpose(2, 0, 1, 3)

    def per_group(members):
        field, coefficient = members
        middle = solve_stream_lines(field, coefficient)
        return middle, solve_normal_lines(middle, coefficient)

    halves, finals = lax.map(per_group, (grouped_velocity, grouped_viscosity))
    half_step = halves.transpose(1, 2, 3, 0, 4).reshape(3, NX, NY, Z)
    advanced = finals.transpose(1, 2, 3, 0, 4).reshape(3, NX, NY, Z)
    return half_step, advanced
```

```python
import jax
import jax.numpy as jnp
from jax import lax
from jax.experimental import pallas as pl
from jax.experimental.pallas import tpu as pltpu
from jax.sharding import PartitionSpec as P

MESH = pl.DeviceIdType.MESH
F32 = jnp.float32


class Network:
    def __init__(self):
        self.edge = {}
        self.ground = {}

    def join(self, a, b, w):
        k = (a, b) if a < b else (b, a)
        self.edge[k] = self.edge[k] + w if k in self.edge else w

    def add_ground(self, a, w):
        self.ground[a] = self.ground[a] + w if a in self.ground else w

    def eliminate(self, k):
        near = {}
        for a, b in list(self.edge):
            if k in (a, b):
                near[b if a == k else a] = self.edge.pop((a, b))
        ground = self.ground.pop(k)
        total = ground
        for w in near.values():
            total = total + w
        inverse = 1.0 / total
        ratio = {a: w * inverse for a, w in near.items()}
        names = sorted(near)
        for i, a in enumerate(names):
            self.add_ground(a, ratio[a] * ground)
            for b in names[i + 1 :]:
                self.join(a, b, ratio[a] * near[b])
        return k, inverse, ratio


def forward(step, source):
    k, inverse, ratio = step
    here = source.pop(k)
    for a, r in ratio.items():
        part = [r * h for h in here]
        source[a] = [s + t for s, t in zip(source[a], part)] if a in source else part
    return [h * inverse for h in here]


def summed(values):
    values = list(values)
    while len(values) > 1:
        values = [
            values[i] + values[i + 1] if i + 1 < len(values) else values[i]
            for i in range(0, len(values), 2)
        ]
    return values[0]


def responses(steps, own, terminals):
    base, unit = {}, {}
    for (k, inverse, ratio), y in reversed(list(zip(steps, own))):
        inner = [(a, r) for a, r in ratio.items() if a not in terminals]
        if y is not None:
            base[k] = [
                summed([y[c]] + [r * base[a][c] for a, r in inner]) for c in range(len(y))
            ]
        unit[k] = {}
        for t in terminals:
            terms = [r * unit[a][t] for a, r in inner if t in unit[a]]
            if t in ratio:
                terms.append(ratio[t])
            if terms:
                unit[k][t] = summed(terms)
    return base, unit


def kernel(
    vel, visc, half, adv,
    xmsg, xin, xret, xback, cmsg, cin, ymsg, yin, yret, yback, send, recv,
):
    gx, gy = lax.axis_index("gx"), lax.axis_index("gy")
    barrier = pltpu.get_barrier_semaphore()
    for axis, me in (("gy", gy), ("gx", gx)):
        for k in range(1, 16):
            pl.semaphore_signal(
                barrier, inc=1, device_id={axis: lax.rem(me + k, 16)}, device_id_type=MESH
            )

    lane_low = lax.broadcasted_iota(jnp.int32, (8, 128), 1) < 64
    row = lax.broadcasted_iota(jnp.int32, (8, 128), 0)

    def turn(x):
        return pltpu.roll(x, 64, 1)

    def pair(q1, q2):
        return jnp.where(lane_low, q1, turn(q2)), jnp.where(lane_low, turn(q1), q2)

    def exchange(axis, me, index, source, target, rows):
        for k in (8, 7, 9, 6, 10, 5, 11, 4, 12, 3, 13, 2, 14, 1, 15):
            peer = lax.rem(me + k, 16)
            pltpu.make_async_remote_copy(
                src_ref=source.at[pl.ds(pl.multiple_of(peer * rows, rows), rows)],
                dst_ref=target.at[pl.ds(pl.multiple_of(me * rows, rows), rows)],
                send_sem=send.at[index],
                recv_sem=recv.at[index],
                device_id={axis: peer},
                device_id_type=MESH,
            ).start()
        mine = pl.ds(pl.multiple_of(me * rows, rows), rows)
        target[mine, :] = source[mine, :]

    def arrived(index, target, rows):
        some = target.at[pl.ds(0, 15 * rows)]
        pltpu.make_async_copy(some, some, recv.at[index]).wait()

    def departed(index, source, rows):
        some = source.at[pl.ds(0, 15 * rows)]
        pltpu.make_async_copy(some, some, send.at[index]).wait()

    nu = [visc[pl.ds(8 * i, 8), :] for i in range(16)]
    net = Network()
    for i in range(16):
        net.add_ground(i, 1.0)
        if i < 15:
            net.join(i, i + 1, (nu[i] + nu[i + 1]) * 0.5)
        if i < 14:
            net.join(i, i + 2, (nu[i] + nu[i + 2]) * 0.125)
    source = {i: [vel[pl.ds(128 * c + 8 * i, 8), :] for c in range(3)] for i in range(16)}
    steps, own = [], []
    for k in (2, 13, 3, 12, 4, 11, 5, 10, 6, 9, 7, 8):
        step = net.eliminate(k)
        steps.append(step)
        own.append(forward(step, source))
    ends = (0, 1, 14, 15)
    out = [net.edge[e] for e in ((0, 1), (0, 14), (0, 15), (1, 14), (1, 15), (14, 15))]
    out += [net.ground[a] for a in ends] + [nu[a] for a in ends]
    out += [source[a][c] for a in ends for c in range(3)]
    for j in range(13):
        for side, value in enumerate(pair(out[2 * j], out[2 * j + 1])):
            xmsg[pl.ds(16 * side + j, 8, stride=32), :] = value
    for side in range(2):
        for j in range(13, 16):
            xmsg[pl.ds(16 * side + j, 8, stride=32), :] = jnp.zeros((8, 128), F32)

    eta = [visc[pl.ds(j, 16, stride=8), :] for j in range(8)]
    net = Network()
    for j in range(8):
        net.add_ground(j, 1.0)
        if j < 7:
            net.join(j, j + 1, eta[j] + eta[j + 1])
    net.add_ground(0, eta[0] * (gy == 0).astype(F32))
    net.add_ground(7, eta[7] * (gy == 15).astype(F32))
    ysteps = [net.eliminate(k) for k in (1, 6, 2, 5, 3, 4)]
    for j, value in enumerate((net.edge[(0, 7)], net.ground[0], net.ground[7], eta[0], eta[7])):
        cmsg[pl.ds(j, 16, stride=8), :] = value
    for j in range(5, 8):
        cmsg[pl.ds(j, 16, stride=8), :] = jnp.zeros((16, 128), F32)
        ymsg[pl.ds(j + (j == 5), 16, stride=8), :] = jnp.zeros((16, 128), F32)
        yret[pl.ds(j + (j == 5), 16, stride=8), :] = jnp.zeros((16, 128), F32)
    for j in range(6, 8):
        for side in range(2):
            xret[pl.ds(64 * side + j, 8, stride=8), :] = jnp.zeros((8, 128), F32)

    pl.semaphore_wait(barrier, 30)
    exchange("gx", gx, 0, xmsg, xin, 16)
    exchange("gy", gy, 1, cmsg, cin, 8)

    xbase, xunit = responses(steps, own, ends)
    unused, yunit = responses(ysteps, [None] * 6, (0, 7))

    arrived(0, xin, 16)
    got = []
    for j in range(13):
        got += pair(xin[pl.ds(j, 8, stride=16), :], xin[pl.ds(128 + j, 8, stride=16), :])
    ring = Network()
    names = ("a", "b", "c", "d")
    for e, (i, j) in enumerate(((0, 1), (0, 2), (0, 3), (1, 2), (1, 3), (2, 3))):
        ring.join(names[i], names[j], got[e])
    for i in range(4):
        ring.add_ground(names[i], got[6 + i])
    rhs = {names[i]: got[14 + 3 * i : 17 + 3 * i] for i in range(4)}
    nu0, nu1, nu14, nu15 = got[10:14]

    def after(x, h, turned=None):
        turned = turn(x) if turned is None else turned
        return turned if h == 8 else pltpu.roll(jnp.where(row >= h, x, turned), 8 - h, 0)

    def before(x, h, turned=None):
        turned = turn(x) if turned is None else turned
        return turned if h == 8 else pltpu.roll(jnp.where(row < 8 - h, x, turned), h, 0)

    last14, last15 = before(nu14, 1), before(nu15, 1)
    ring.join("a", "q", (last15 + nu0) * 0.5)
    ring.join("a", "p", (last14 + nu0) * 0.125)
    ring.join("b", "q", (last15 + nu1) * 0.125)
    rsteps = [ring.eliminate("a")]
    rown = [forward(rsteps[0], rhs)]
    rsteps.append(ring.eliminate("b"))
    rown.append(forward(rsteps[1], rhs))
    behind = [[ring.edge[("c", "p")], ring.edge[("c", "q")]], [ring.edge[("d", "p")], ring.edge[("d", "q")]]]
    onward = [[after(behind[j][i], 1) for j in range(2)] for i in range(2)]
    ground = [ring.ground["c"] + after(ring.ground["p"], 1), ring.ground["d"] + after(ring.ground["q"], 1)]
    inner = ring.edge[("c", "d")] + after(ring.edge[("p", "q")], 1)
    field = [
        [rhs[n][c] + after(rhs[m][c], 1) for c in range(3)] for n, m in (("c", "p"), ("d", "q"))
    ]

    def block_inverse(rest, link):
        scale = 1.0 / (rest[0] * rest[1] + link * (rest[0] + rest[1]))
        cross = link * scale
        return [[rest[1] * scale + cross, cross], [cross, rest[0] * scale + cross]]

    def times(m, v):
        return [[m[i][0] * v[0][j] + m[i][1] * v[1][j] for j in range(len(v[0]))] for i in range(2)]

    for h in (1, 2, 4):
        rest = [
            ground[i] + ((behind[i][0] + behind[i][1]) + (onward[i][0] + onward[i][1]))
            for i in range(2)
        ]
        inv = block_inverse(rest, inner)
        solved = times(inv, [[ground[i]] + field[i] + behind[i] + onward[i] for i in range(2)])
        turned = [[turn(x) for x in line] for line in solved]
        up = [[after(x, h, t) for x, t in zip(l, tl)] for l, tl in zip(solved, turned)]
        down = [[before(x, h, t) for x, t in zip(l, tl)] for l, tl in zip(solved, turned)]
        from_up, from_down = times(onward, up), times(behind, down)
        ground = [ground[i] + from_up[i][0] + from_down[i][0] for i in range(2)]
        field = [
            [field[i][c] + from_up[i][1 + c] + from_down[i][1 + c] for c in range(3)]
            for i in range(2)
        ]
        inner = inner + from_up[0][5] + from_down[0][7]
        onward = [from_up[i][6:8] for i in range(2)]
        behind = [from_down[i][4:6] for i in range(2)]
    across = [[behind[i][j] + onward[i][j] for j in range(2)] for i in range(2)]
    rest = [ground[i] + (across[i][0] + across[i][1]) for i in range(2)]
    inv = block_inverse(rest, inner)
    solved = times(inv, [[ground[i]] + field[i] + [across[i][1]] for i in range(2)])
    other = times(across, [[turn(x) for x in line] for line in solved])
    ground = [ground[i] + other[i][0] for i in range(2)]
    field = [[field[i][c] + other[i][1 + c] for c in range(3)] for i in range(2)]
    inner = inner + other[0][4]
    value_c, value_d = times(block_inverse(ground, inner), field)
    value = {"c": value_c, "d": value_d}
    value["p"] = [before(x, 1) for x in value_c]
    value["q"] = [before(x, 1) for x in value_d]
    for (k, unused, ratio), y in zip(rsteps[::-1], rown[::-1]):
        value[k] = [summed([y[c]] + [r * value[a][c] for a, r in ratio.items()]) for c in range(3)]
    out = [value[n][c] for n in names for c in range(3)]
    for j in range(6):
        for side, line in enumerate(pair(out[2 * j], out[2 * j + 1])):
            xret[pl.ds(64 * side + j, 8, stride=8), :] = line
    exchange("gx", gx, 2, xret, xback, 8)

    arrived(1, cin, 8)
    link, ground_a, ground_b, eta0, eta7 = [cin[pl.ds(j, 16, stride=8), :] for j in range(5)]
    segment = lax.broadcasted_iota(jnp.int32, (16, 128), 0)

    def lower(x, h):
        return pltpu.roll(x, h, 0)

    def upper(x, h):
        return pltpu.roll(x, 16 - h, 0)

    gate = jnp.where(segment == 0, 0.0, lower(eta7, 1) + eta0)
    inverse_a = 1.0 / (ground_a + link + gate)
    to_b, to_q = link * inverse_a, gate * inverse_a
    low = to_q * link
    high = jnp.where(segment == 15, 0.0, upper(low, 1))
    to_b_up = jnp.where(segment == 15, 0.0, upper(to_q, 1))
    ground = ground_b + to_b * ground_a + to_b_up * upper(ground_a, 1)
    sweeps = []
    for h in (1, 2, 4, 8):
        inverse = 1.0 / (ground + low + high)
        weight_low, weight_high = low * lower(inverse, h), high * upper(inverse, h)
        sweeps.append((h, weight_low, weight_high))
        ground = ground + weight_low * lower(ground, h) + weight_high * upper(ground, h)
        low, high = weight_low * lower(low, h), weight_high * upper(high, h)
    inverse_b = 1.0 / ground

    arrived(2, xback, 8)
    got = []
    for j in range(6):
        got += pair(xback[pl.ds(j, 8, stride=16), :], xback[pl.ds(8 + j, 8, stride=16), :])
    value = {a: got[3 * i : 3 * i + 3] for i, a in enumerate(ends)}
    for i in range(16):
        for c in range(3):
            if i in ends:
                x = value[i][c]
            else:
                x = summed([xbase[i][c]] + [w * value[a][c] for a, w in xunit[i].items()])
            half[pl.ds(128 * c + 8 * i, 8), :] = x

    lines = [[half[pl.ds(128 * c + j, 16, stride=8), :] for c in range(3)] for j in range(8)]
    for i, end in enumerate((0, 7)):
        for c in range(3):
            ymsg[pl.ds(3 * i + c, 16, stride=8), :] = summed(
                [lines[end][c]] + [yunit[k][end] * lines[k][c] for k in range(1, 7) if end in yunit[k]]
            )
    exchange("gy", gy, 3, ymsg, yin, 8)
    source = {j: list(lines[j]) for j in range(8)}
    yown = [forward(step, source) for step in ysteps]
    ybase, unused = responses(ysteps, yown, (0, 7))

    arrived(3, yin, 8)
    ends_a = [yin[pl.ds(c, 16, stride=8), :] for c in range(3)]
    ends_b = [yin[pl.ds(3 + c, 16, stride=8), :] for c in range(3)]
    for c in range(3):
        f = ends_b[c] + to_b * ends_a[c] + to_b_up * upper(ends_a[c], 1)
        for h, weight_low, weight_high in sweeps:
            f = f + weight_low * lower(f, h) + weight_high * upper(f, h)
        f = f * inverse_b
        yret[pl.ds(3 + c, 16, stride=8), :] = f
        yret[pl.ds(c, 16, stride=8), :] = inverse_a * ends_a[c] + to_b * f + to_q * lower(f, 1)
    exchange("gy", gy, 4, yret, yback, 8)

    arrived(4, yback, 8)
    first = [yback[pl.ds(c, 16, stride=8), :] for c in range(3)]
    final = [yback[pl.ds(3 + c, 16, stride=8), :] for c in range(3)]
    for c in range(3):
        for j in range(8):
            if j == 0:
                x = first[c]
            elif j == 7:
                x = final[c]
            else:
                x = ybase[j][c] + (yunit[j][0] * first[c] + yunit[j][7] * final[c])
            adv[pl.ds(128 * c + j, 16, stride=8), :] = x

    departed(0, xmsg, 16)
    departed(1, cmsg, 8)
    departed(2, xret, 8)
    departed(3, ymsg, 8)
    departed(4, yret, 8)


def on_device(velocity, viscosity):
    vmem = pl.BlockSpec(memory_space=pltpu.VMEM)
    small, large = pltpu.VMEM((128, 128), F32), pltpu.VMEM((256, 128), F32)
    half, adv = pl.pallas_call(
        kernel,
        name="adi",
        out_shape=[jax.ShapeDtypeStruct((384, 128), F32)] * 2,
        in_specs=[vmem, vmem],
        out_specs=[vmem, vmem],
        scratch_shapes=[large, large] + [small] * 8
        + [pltpu.SemaphoreType.DMA((5,)), pltpu.SemaphoreType.DMA((5,))],
        compiler_params=pltpu.CompilerParams(
            collective_id=0, has_side_effects=True, vmem_limit_bytes=32 * 1024 * 1024
        ),
    )(velocity.reshape(384, 128), viscosity.reshape(128, 128))
    return half.reshape(velocity.shape), adv.reshape(velocity.shape)


def solution(mesh):
    return jax.shard_map(
        on_device,
        mesh=mesh,
        in_specs=(P(None, "gx", "gy", None), P("gx", "gy", None)),
        out_specs=(P(None, "gx", "gy", None), P(None, "gx", "gy", None)),
        check_vma=False,
    )
```

```python
import jax
import jax.numpy as jnp
from jax import lax
from jax.experimental import pallas as pl
from jax.experimental.pallas import tpu as pltpu
from jax.sharding import PartitionSpec as P

MESH = pl.DeviceIdType.MESH
F32 = jnp.float32


class Network:
    def __init__(self):
        self.edge = {}
        self.ground = {}

    def join(self, a, b, w):
        k = (a, b) if a < b else (b, a)
        self.edge[k] = self.edge[k] + w if k in self.edge else w

    def add_ground(self, a, w):
        self.ground[a] = self.ground[a] + w if a in self.ground else w

    def eliminate(self, k):
        near = {}
        for a, b in list(self.edge):
            if k in (a, b):
                near[b if a == k else a] = self.edge.pop((a, b))
        ground = self.ground.pop(k)
        total = ground
        for w in near.values():
            total = total + w
        inverse = 1.0 / total
        ratio = {a: w * inverse for a, w in near.items()}
        names = sorted(near)
        for i, a in enumerate(names):
            self.add_ground(a, ratio[a] * ground)
            for b in names[i + 1 :]:
                self.join(a, b, ratio[a] * near[b])
        return k, inverse, ratio


def forward(step, source):
    k, inverse, ratio = step
    here = source.pop(k)
    for a, r in ratio.items():
        part = [r * h for h in here]
        source[a] = [s + t for s, t in zip(source[a], part)] if a in source else part
    return [h * inverse for h in here]


def summed(values):
    values = list(values)
    while len(values) > 1:
        values = [
            values[i] + values[i + 1] if i + 1 < len(values) else values[i]
            for i in range(0, len(values), 2)
        ]
    return values[0]


def responses(steps, own, terminals):
    base, unit = {}, {}
    for (k, inverse, ratio), y in reversed(list(zip(steps, own))):
        inner = [(a, r) for a, r in ratio.items() if a not in terminals]
        if y is not None:
            base[k] = [
                summed([y[c]] + [r * base[a][c] for a, r in inner]) for c in range(len(y))
            ]
        unit[k] = {}
        for t in terminals:
            terms = [r * unit[a][t] for a, r in inner if t in unit[a]]
            if t in ratio:
                terms.append(ratio[t])
            if terms:
                unit[k][t] = summed(terms)
    return base, unit


def kernel(
    vel_hbm, visc_hbm, half, adv,
    vel, visc, load, xmsg, xin, xret, xback, cmsg, cin, ymsg, yin, yret, yback, send, recv, near, far,
):
    gx, gy = lax.axis_index("gx"), lax.axis_index("gy")
    barrier = pltpu.get_barrier_semaphore()
    def place(side, move):
        return lax.rem(gy // 8 + side, 2) * 8 + lax.rem(gy + 8 + move, 8)

    def tell(semaphore, axis, peer):
        pl.semaphore_signal(semaphore, inc=1, device_id={axis: peer}, device_id_type=MESH)

    for peer in (place(0, 1), place(0, -1), place(1, 0), place(1, 1), place(1, -1)):
        tell(barrier, "gy", peer)
    for k in range(1, 16):
        tell(barrier, "gx", lax.rem(gx + k, 16))

    loads = [
        pltpu.make_async_copy(visc_hbm, visc, load.at[0]),
        pltpu.make_async_copy(vel_hbm, vel, load.at[1]),
    ]
    for copy in loads:
        copy.start()

    lane_low = lax.broadcasted_iota(jnp.int32, (8, 128), 1) < 64
    row = lax.broadcasted_iota(jnp.int32, (8, 128), 0)

    def turn(x):
        return pltpu.roll(x, 64, 1)

    def pair(q1, q2):
        return jnp.where(lane_low, q1, turn(q2)), jnp.where(lane_low, turn(q1), q2)

    def exchange(axis, me, index, source, target, rows):
        for k in (8, 7, 9, 6, 10, 5, 11, 4, 12, 3, 13, 2, 14, 1, 15):
            peer = lax.rem(me + k, 16)
            pltpu.make_async_remote_copy(
                src_ref=source.at[pl.ds(pl.multiple_of(peer * rows, rows), rows)],
                dst_ref=target.at[pl.ds(pl.multiple_of(me * rows, rows), rows)],
                send_sem=send.at[index],
                recv_sem=recv.at[index],
                device_id={axis: peer},
                device_id_type=MESH,
            ).start()
        mine = pl.ds(pl.multiple_of(me * rows, rows), rows)
        target[mine, :] = source[mine, :]

    def arrived(index, target, rows):
        some = target.at[pl.ds(0, 15 * rows)]
        pltpu.make_async_copy(some, some, recv.at[index]).wait()

    def departed(index, source, rows):
        some = source.at[pl.ds(0, 15 * rows)]
        pltpu.make_async_copy(some, some, send.at[index]).wait()

    for copy in loads:
        copy.wait()

    nu = [visc[pl.ds(8 * i, 8), :] for i in range(16)]
    net = Network()
    for i in range(16):
        net.add_ground(i, 1.0)
        if i < 15:
            net.join(i, i + 1, (nu[i] + nu[i + 1]) * 0.5)
        if i < 14:
            net.join(i, i + 2, (nu[i] + nu[i + 2]) * 0.125)
    source = {i: [vel[pl.ds(128 * c + 8 * i, 8), :] for c in range(3)] for i in range(16)}
    steps, own = [], []
    for k in (2, 13, 3, 12, 4, 11, 5, 10, 6, 9, 7, 8):
        step = net.eliminate(k)
        steps.append(step)
        own.append(forward(step, source))
    ends = (0, 1, 14, 15)
    out = [net.edge[e] for e in ((0, 1), (0, 14), (0, 15), (1, 14), (1, 15), (14, 15))]
    out += [net.ground[a] for a in ends] + [nu[a] for a in ends]
    out += [source[a][c] for a in ends for c in range(3)]
    for j in range(13):
        for side, value in enumerate(pair(out[2 * j], out[2 * j + 1])):
            xmsg[pl.ds(16 * side + j, 8, stride=32), :] = value
    for side in range(2):
        for j in range(13, 16):
            xmsg[pl.ds(16 * side + j, 8, stride=32), :] = jnp.zeros((8, 128), F32)

    eta = [visc[pl.ds(j, 16, stride=8), :] for j in range(8)]
    net = Network()
    for j in range(8):
        net.add_ground(j, 1.0)
        if j < 7:
            net.join(j, j + 1, eta[j] + eta[j + 1])
    net.add_ground(0, eta[0] * (gy == 0).astype(F32))
    net.add_ground(7, eta[7] * (gy == 15).astype(F32))
    ysteps = [net.eliminate(k) for k in (1, 6, 2, 5, 3, 4)]
    for j, value in enumerate((net.edge[(0, 7)], net.ground[0], net.ground[7], eta[0], eta[7])):
        cmsg[pl.ds(j, 16, stride=8), :] = value
    for j in range(5, 8):
        cmsg[pl.ds(j, 16, stride=8), :] = jnp.zeros((16, 128), F32)
        ymsg[pl.ds(j + (j == 5), 16, stride=8), :] = jnp.zeros((16, 128), F32)
        yret[pl.ds(j + (j == 5), 16, stride=8), :] = jnp.zeros((16, 128), F32)
    for j in range(6, 8):
        for side in range(2):
            xret[pl.ds(64 * side + j, 8, stride=8), :] = jnp.zeros((8, 128), F32)

    pl.semaphore_wait(barrier, 20)
    exchange("gx", gx, 0, xmsg, xin, 16)
    tell(near, "gy", place(0, 1))
    tell(near, "gy", place(0, -1))

    xbase, xunit = responses(steps, own, ends)
    unused, yunit = responses(ysteps, [None] * 6, (0, 7))

    pl.semaphore_wait(near, 2)
    tell(far, "gy", place(0, 2))
    tell(far, "gy", place(0, -2))

    arrived(0, xin, 16)
    got = []
    for j in range(13):
        got += pair(xin[pl.ds(j, 8, stride=16), :], xin[pl.ds(128 + j, 8, stride=16), :])
    ring = Network()
    names = ("a", "b", "c", "d")
    for e, (i, j) in enumerate(((0, 1), (0, 2), (0, 3), (1, 2), (1, 3), (2, 3))):
        ring.join(names[i], names[j], got[e])
    for i in range(4):
        ring.add_ground(names[i], got[6 + i])
    rhs = {names[i]: got[14 + 3 * i : 17 + 3 * i] for i in range(4)}
    nu0, nu1, nu14, nu15 = got[10:14]

    def after(x, h, turned=None):
        turned = turn(x) if turned is None else turned
        return turned if h == 8 else pltpu.roll(jnp.where(row >= h, x, turned), 8 - h, 0)

    def before(x, h, turned=None):
        turned = turn(x) if turned is None else turned
        return turned if h == 8 else pltpu.roll(jnp.where(row < 8 - h, x, turned), h, 0)

    last14, last15 = before(nu14, 1), before(nu15, 1)
    ring.join("a", "q", (last15 + nu0) * 0.5)
    ring.join("a", "p", (last14 + nu0) * 0.125)
    ring.join("b", "q", (last15 + nu1) * 0.125)
    rsteps = [ring.eliminate("a")]
    rown = [forward(rsteps[0], rhs)]
    rsteps.append(ring.eliminate("b"))
    rown.append(forward(rsteps[1], rhs))
    behind = [[ring.edge[("c", "p")], ring.edge[("c", "q")]], [ring.edge[("d", "p")], ring.edge[("d", "q")]]]
    onward = [[after(behind[j][i], 1) for j in range(2)] for i in range(2)]
    ground = [ring.ground["c"] + after(ring.ground["p"], 1), ring.ground["d"] + after(ring.ground["q"], 1)]
    inner = ring.edge[("c", "d")] + after(ring.edge[("p", "q")], 1)
    field = [
        [rhs[n][c] + after(rhs[m][c], 1) for c in range(3)] for n, m in (("c", "p"), ("d", "q"))
    ]

    def block_inverse(rest, link):
        scale = 1.0 / (rest[0] * rest[1] + link * (rest[0] + rest[1]))
        cross = link * scale
        return [[rest[1] * scale + cross, cross], [cross, rest[0] * scale + cross]]

    def times(m, v):
        return [[m[i][0] * v[0][j] + m[i][1] * v[1][j] for j in range(len(v[0]))] for i in range(2)]

    for h in (1, 2, 4):
        rest = [
            ground[i] + ((behind[i][0] + behind[i][1]) + (onward[i][0] + onward[i][1]))
            for i in range(2)
        ]
        inv = block_inverse(rest, inner)
        solved = times(inv, [[ground[i]] + field[i] + behind[i] + onward[i] for i in range(2)])
        turned = [[turn(x) for x in line] for line in solved]
        up = [[after(x, h, t) for x, t in zip(l, tl)] for l, tl in zip(solved, turned)]
        down = [[before(x, h, t) for x, t in zip(l, tl)] for l, tl in zip(solved, turned)]
        from_up, from_down = times(onward, up), times(behind, down)
        ground = [ground[i] + from_up[i][0] + from_down[i][0] for i in range(2)]
        field = [
            [field[i][c] + from_up[i][1 + c] + from_down[i][1 + c] for c in range(3)]
            for i in range(2)
        ]
        inner = inner + from_up[0][5] + from_down[0][7]
        onward = [from_up[i][6:8] for i in range(2)]
        behind = [from_down[i][4:6] for i in range(2)]
    across = [[behind[i][j] + onward[i][j] for j in range(2)] for i in range(2)]
    rest = [ground[i] + (across[i][0] + across[i][1]) for i in range(2)]
    inv = block_inverse(rest, inner)
    solved = times(inv, [[ground[i]] + field[i] + [across[i][1]] for i in range(2)])
    other = times(across, [[turn(x) for x in line] for line in solved])
    ground = [ground[i] + other[i][0] for i in range(2)]
    field = [[field[i][c] + other[i][1 + c] for c in range(3)] for i in range(2)]
    inner = inner + other[0][4]
    value_c, value_d = times(block_inverse(ground, inner), field)
    value = {"c": value_c, "d": value_d}
    value["p"] = [before(x, 1) for x in value_c]
    value["q"] = [before(x, 1) for x in value_d]
    for (k, unused, ratio), y in zip(rsteps[::-1], rown[::-1]):
        value[k] = [summed([y[c]] + [r * value[a][c] for a, r in ratio.items()]) for c in range(3)]
    out = [value[n][c] for n in names for c in range(3)]
    for j in range(6):
        for side, line in enumerate(pair(out[2 * j], out[2 * j + 1])):
            xret[pl.ds(64 * side + j, 8, stride=8), :] = line
    exchange("gx", gx, 2, xret, xback, 8)
    pl.semaphore_wait(far, 2)
    exchange("gy", gy, 1, cmsg, cin, 8)

    arrived(2, xback, 8)
    got = []
    for j in range(6):
        got += pair(xback[pl.ds(j, 8, stride=16), :], xback[pl.ds(8 + j, 8, stride=16), :])
    value = {a: got[3 * i : 3 * i + 3] for i, a in enumerate(ends)}
    for i in range(16):
        for c in range(3):
            if i in ends:
                x = value[i][c]
            else:
                x = summed([xbase[i][c]] + [w * value[a][c] for a, w in xunit[i].items()])
            half[pl.ds(128 * c + 8 * i, 8), :] = x

    lines = [[half[pl.ds(128 * c + j, 16, stride=8), :] for c in range(3)] for j in range(8)]
    for i, end in enumerate((0, 7)):
        for c in range(3):
            ymsg[pl.ds(3 * i + c, 16, stride=8), :] = summed(
                [lines[end][c]] + [yunit[k][end] * lines[k][c] for k in range(1, 7) if end in yunit[k]]
            )
    exchange("gy", gy, 3, ymsg, yin, 8)
    source = {j: list(lines[j]) for j in range(8)}
    yown = [forward(step, source) for step in ysteps]
    ybase, unused = responses(ysteps, yown, (0, 7))

    arrived(1, cin, 8)
    link, ground_a, ground_b, eta0, eta7 = [cin[pl.ds(j, 16, stride=8), :] for j in range(5)]
    segment = lax.broadcasted_iota(jnp.int32, (16, 128), 0)

    def lower(x, h):
        return pltpu.roll(x, h, 0)

    def upper(x, h):
        return pltpu.roll(x, 16 - h, 0)

    gate = jnp.where(segment == 0, 0.0, lower(eta7, 1) + eta0)
    inverse_a = 1.0 / (ground_a + link + gate)
    to_b, to_q = link * inverse_a, gate * inverse_a
    low = to_q * link
    high = jnp.where(segment == 15, 0.0, upper(low, 1))
    to_b_up = jnp.where(segment == 15, 0.0, upper(to_q, 1))
    ground = ground_b + to_b * ground_a + to_b_up * upper(ground_a, 1)
    sweeps = []
    for h in (1, 2, 4, 8):
        inverse = 1.0 / (ground + low + high)
        weight_low, weight_high = low * lower(inverse, h), high * upper(inverse, h)
        sweeps.append((h, weight_low, weight_high))
        ground = ground + weight_low * lower(ground, h) + weight_high * upper(ground, h)
        low, high = weight_low * lower(low, h), weight_high * upper(high, h)
    inverse_b = 1.0 / ground

    arrived(3, yin, 8)
    ends_a = [yin[pl.ds(c, 16, stride=8), :] for c in range(3)]
    ends_b = [yin[pl.ds(3 + c, 16, stride=8), :] for c in range(3)]
    for c in range(3):
        f = ends_b[c] + to_b * ends_a[c] + to_b_up * upper(ends_a[c], 1)
        for h, weight_low, weight_high in sweeps:
            f = f + weight_low * lower(f, h) + weight_high * upper(f, h)
        f = f * inverse_b
        yret[pl.ds(3 + c, 16, stride=8), :] = f
        yret[pl.ds(c, 16, stride=8), :] = inverse_a * ends_a[c] + to_b * f + to_q * lower(f, 1)
    exchange("gy", gy, 4, yret, yback, 8)

    arrived(4, yback, 8)
    first = [yback[pl.ds(c, 16, stride=8), :] for c in range(3)]
    final = [yback[pl.ds(3 + c, 16, stride=8), :] for c in range(3)]
    for c in range(3):
        for j in range(8):
            if j == 0:
                x = first[c]
            elif j == 7:
                x = final[c]
            else:
                x = ybase[j][c] + (yunit[j][0] * first[c] + yunit[j][7] * final[c])
            adv[pl.ds(128 * c + j, 16, stride=8), :] = x

    departed(0, xmsg, 16)
    departed(1, cmsg, 8)
    departed(2, xret, 8)
    departed(3, ymsg, 8)
    departed(4, yret, 8)


def store(half, adv, half_hbm, adv_hbm, done):
    copies = [
        pltpu.make_async_copy(half, half_hbm, done.at[0]),
        pltpu.make_async_copy(adv, adv_hbm, done.at[1]),
    ]
    for copy in copies:
        copy.start()
    for copy in copies:
        copy.wait()


def on_device(velocity, viscosity):
    vmem, hbm = pl.BlockSpec(memory_space=pltpu.VMEM), pl.BlockSpec(memory_space=pltpu.HBM)
    small, large = pltpu.VMEM((128, 128), F32), pltpu.VMEM((256, 128), F32)
    held = [
        pltpu.with_memory_space_constraint(x, pltpu.HBM)
        for x in (velocity.reshape(384, 128), viscosity.reshape(128, 128))
    ]
    half, adv = pl.pallas_call(
        kernel,
        name="adi",
        out_shape=[jax.ShapeDtypeStruct((384, 128), F32)] * 2,
        in_specs=[hbm, hbm],
        out_specs=[vmem, vmem],
        scratch_shapes=[pltpu.VMEM((384, 128), F32), small, pltpu.SemaphoreType.DMA((2,)), large, large] + [small] * 8
        + [pltpu.SemaphoreType.DMA((5,)), pltpu.SemaphoreType.DMA((5,))]
        + [pltpu.SemaphoreType.REGULAR] * 2,
        compiler_params=pltpu.CompilerParams(
            collective_id=0, has_side_effects=True, vmem_limit_bytes=32 * 1024 * 1024
        ),
    )(*held)
    half, adv = pl.pallas_call(
        store,
        name="store",
        out_shape=[jax.ShapeDtypeStruct((384, 128), F32)] * 2,
        in_specs=[vmem, vmem],
        out_specs=[hbm, hbm],
        scratch_shapes=[pltpu.SemaphoreType.DMA((2,))],
        compiler_params=pltpu.CompilerParams(vmem_limit_bytes=1024 * 1024),
    )(half, adv)
    return half.reshape(velocity.shape), adv.reshape(velocity.shape)


def solution(mesh):
    return jax.shard_map(
        on_device,
        mesh=mesh,
        in_specs=(P(None, "gx", "gy", None), P("gx", "gy", None)),
        out_specs=(P(None, "gx", "gy", None), P(None, "gx", "gy", None)),
        check_vma=False,
    )
```

```python
import jax
import jax.numpy as jnp
from jax import lax
from jax.experimental import pallas as pl
from jax.experimental.pallas import tpu as pltpu
from jax.sharding import PartitionSpec as P

MESH = pl.DeviceIdType.MESH
F32 = jnp.float32


class Network:
    def __init__(self):
        self.edge = {}
        self.ground = {}

    def join(self, a, b, w):
        k = (a, b) if a < b else (b, a)
        self.edge[k] = self.edge[k] + w if k in self.edge else w

    def add_ground(self, a, w):
        self.ground[a] = self.ground[a] + w if a in self.ground else w

    def eliminate(self, k):
        near = {}
        for a, b in list(self.edge):
            if k in (a, b):
                near[b if a == k else a] = self.edge.pop((a, b))
        ground = self.ground.pop(k)
        total = ground
        for w in near.values():
            total = total + w
        inverse = 1.0 / total
        ratio = {a: w * inverse for a, w in near.items()}
        names = sorted(near)
        for i, a in enumerate(names):
            self.add_ground(a, ratio[a] * ground)
            for b in names[i + 1 :]:
                self.join(a, b, ratio[a] * near[b])
        return k, inverse, ratio


def forward(step, source):
    k, inverse, ratio = step
    here = source.pop(k)
    for a, r in ratio.items():
        part = [r * h for h in here]
        source[a] = [s + t for s, t in zip(source[a], part)] if a in source else part
    return [h * inverse for h in here]


def summed(values):
    values = list(values)
    while len(values) > 1:
        values = [
            values[i] + values[i + 1] if i + 1 < len(values) else values[i]
            for i in range(0, len(values), 2)
        ]
    return values[0]


def responses(steps, own, terminals):
    base, unit = {}, {}
    for (k, inverse, ratio), y in reversed(list(zip(steps, own))):
        inner = [(a, r) for a, r in ratio.items() if a not in terminals]
        if y is not None:
            base[k] = [
                summed([y[c]] + [r * base[a][c] for a, r in inner]) for c in range(len(y))
            ]
        unit[k] = {}
        for t in terminals:
            terms = [r * unit[a][t] for a, r in inner if t in unit[a]]
            if t in ratio:
                terms.append(ratio[t])
            if terms:
                unit[k][t] = summed(terms)
    return base, unit


def kernel(
    vel_hbm, visc_hbm, half, adv,
    vel, visc, load, xmsg, xin, xret, xback, cmsg, cin, ymsg, yin, yret, yback, send, recv, near, far, wide, go,
):
    gx, gy = lax.axis_index("gx"), lax.axis_index("gy")
    barrier = pltpu.get_barrier_semaphore()
    def place(side, move):
        return lax.rem(gy // 8 + side, 2) * 8 + lax.rem(gy + 8 + move, 8)

    def tell(semaphore, axis, peer):
        pl.semaphore_signal(semaphore, inc=1, device_id={axis: peer}, device_id_type=MESH)

    chip, core = gx // 2, lax.rem(gx, 2)

    around = (place(1, 1), place(1, -1), place(1, 0), place(0, 1), place(0, -1))

    @pl.when(core == 1)
    def announce():
        for peer in around:
            tell(barrier, "gy", peer)
        for k in (12, 4, 13, 11, 5, 3, 14, 10, 6, 2, 9, 7, 8, 1, 15):
            tell(barrier, "gx", lax.rem(gx + k, 16))

    @pl.when(core == 0)
    def report():
        tell(barrier, "gx", gx + 1)

    loads = [
        pltpu.make_async_copy(visc_hbm, visc, load.at[0]),
        pltpu.make_async_copy(vel_hbm, vel, load.at[1]),
    ]
    for copy in loads:
        copy.start()

    def push(index, source, start, target, to, rows, **place):
        pltpu.make_async_remote_copy(
            src_ref=source.at[pl.ds(pl.multiple_of(start, 8), rows)],
            dst_ref=target.at[pl.ds(pl.multiple_of(to, 8), rows)],
            send_sem=send.at[index],
            recv_sem=recv.at[index],
            device_id=place,
            device_id_type=MESH,
        ).start()

    def exchange(index, source, target):
        for k in (8, 7, 9, 6, 10, 5, 11, 4, 12, 3, 13, 2, 14, 1, 15):
            peer = lax.rem(gy + k, 16)
            push(index, source, peer * 8, target, gy * 8, 8, gy=peer)
        mine = pl.ds(pl.multiple_of(gy * 8, 8), 8)
        target[mine, :] = source[mine, :]

    def arrived(index, target, rows):
        some = target.at[pl.ds(0, rows)]
        pltpu.make_async_copy(some, some, recv.at[index]).wait()

    def departed(index, source, rows):
        some = source.at[pl.ds(0, rows)]
        pltpu.make_async_copy(some, some, send.at[index]).wait()

    for copy in loads:
        copy.wait()

    nu = [visc[pl.ds(8 * i, 8), :] for i in range(16)]
    net = Network()
    for i in range(16):
        net.add_ground(i, 1.0)
        if i < 15:
            net.join(i, i + 1, (nu[i] + nu[i + 1]) * 0.5)
        if i < 14:
            net.join(i, i + 2, (nu[i] + nu[i + 2]) * 0.125)
    source = {i: [vel[pl.ds(128 * c + 8 * i, 8), :] for c in range(3)] for i in range(16)}
    steps, own = [], []
    for k in (2, 13, 3, 12, 4, 11, 5, 10, 6, 9, 7, 8):
        step = net.eliminate(k)
        steps.append(step)
        own.append(forward(step, source))
    ends = (0, 1, 14, 15)
    out = [net.edge[e] for e in ((0, 1), (0, 14), (0, 15), (1, 14), (1, 15), (14, 15))]
    out += [net.ground[a] for a in ends] + [nu[a] for a in ends]
    out += [source[a][c] for a in ends for c in range(3)]
    for j, value in enumerate(out):
        xmsg[pl.ds(j, 8, stride=32), :] = value

    eta = [visc[pl.ds(j, 16, stride=8), :] for j in range(8)]
    net = Network()
    for j in range(8):
        net.add_ground(j, 1.0)
        if j < 7:
            net.join(j, j + 1, eta[j] + eta[j + 1])
    net.add_ground(0, eta[0] * (gy == 0).astype(F32))
    net.add_ground(7, eta[7] * (gy == 15).astype(F32))
    ysteps = [net.eliminate(k) for k in (1, 6, 2, 5, 3, 4)]
    for j, value in enumerate((net.edge[(0, 7)], net.ground[0], net.ground[7], eta[0], eta[7])):
        cmsg[pl.ds(j, 16, stride=8), :] = value
    for j in range(5, 8):
        cmsg[pl.ds(j, 16, stride=8), :] = jnp.zeros((16, 128), F32)
        ymsg[pl.ds(j + (j == 5), 16, stride=8), :] = jnp.zeros((16, 128), F32)
        yret[pl.ds(j + (j == 5), 16, stride=8), :] = jnp.zeros((16, 128), F32)

    pl.semaphore_wait(barrier, 8 + 5 * core)
    for k in (4, 3, 5, 2, 6, 1, 7):
        peer = lax.rem(chip + k, 8)
        push(0, xmsg, peer * 32, xin, gx * 32, 26, gx=peer * 2 + 1)

    @pl.when(core == 0)
    def lend():
        push(0, xmsg, chip * 32, xin, gx * 32, 26, gx=gx + 1)

    @pl.when(core == 1)
    def keep():
        for peer in around:
            tell(near, "gy", peer)
        xin[pl.ds(pl.multiple_of(gx * 32, 8), 26), :] = xmsg[
            pl.ds(pl.multiple_of(chip * 32, 8), 26), :
        ]

    xbase, xunit = responses(steps, own, ends)
    unused, yunit = responses(ysteps, [None] * 6, (0, 7))

    @pl.when(core == 1)
    def solve_ring():
        pl.semaphore_wait(near, 5)
        tell(far, "gy", place(0, 2))
        tell(far, "gy", place(0, -2))

        arrived(0, xin, 15 * 26)
        got = [xin[pl.ds(j, 16, stride=32), :] for j in range(26)]
        ring = Network()
        names = ("a", "b", "c", "d")
        for e, (i, j) in enumerate(((0, 1), (0, 2), (0, 3), (1, 2), (1, 3), (2, 3))):
            ring.join(names[i], names[j], got[e])
        for i in range(4):
            ring.add_ground(names[i], got[6 + i])
        rhs = {names[i]: got[14 + 3 * i : 17 + 3 * i] for i in range(4)}
        nu0, nu1, nu14, nu15 = got[10:14]

        def after(x, h):
            return pltpu.roll(x, 16 - h, 0)

        def before(x, h):
            return pltpu.roll(x, h, 0)

        last14, last15 = before(nu14, 1), before(nu15, 1)
        ring.join("a", "q", (last15 + nu0) * 0.5)
        ring.join("a", "p", (last14 + nu0) * 0.125)
        ring.join("b", "q", (last15 + nu1) * 0.125)
        rsteps = [ring.eliminate("a")]
        rown = [forward(rsteps[0], rhs)]
        rsteps.append(ring.eliminate("b"))
        rown.append(forward(rsteps[1], rhs))
        behind = [[ring.edge[("c", "p")], ring.edge[("c", "q")]], [ring.edge[("d", "p")], ring.edge[("d", "q")]]]
        onward = [[after(behind[j][i], 1) for j in range(2)] for i in range(2)]
        ground = [ring.ground["c"] + after(ring.ground["p"], 1), ring.ground["d"] + after(ring.ground["q"], 1)]
        inner = ring.edge[("c", "d")] + after(ring.edge[("p", "q")], 1)
        field = [
            [rhs[n][c] + after(rhs[m][c], 1) for c in range(3)] for n, m in (("c", "p"), ("d", "q"))
        ]

        def block_inverse(rest, link):
            scale = 1.0 / (rest[0] * rest[1] + link * (rest[0] + rest[1]))
            cross = link * scale
            return [[rest[1] * scale + cross, cross], [cross, rest[0] * scale + cross]]

        def times(m, v):
            return [[m[i][0] * v[0][j] + m[i][1] * v[1][j] for j in range(len(v[0]))] for i in range(2)]

        for h in (1, 2, 4):
            rest = [
                ground[i] + ((behind[i][0] + behind[i][1]) + (onward[i][0] + onward[i][1]))
                for i in range(2)
            ]
            inv = block_inverse(rest, inner)
            solved = times(inv, [[ground[i]] + field[i] + behind[i] + onward[i] for i in range(2)])
            up = [[after(x, h) for x in line] for line in solved]
            down = [[before(x, h) for x in line] for line in solved]
            from_up, from_down = times(onward, up), times(behind, down)
            ground = [ground[i] + from_up[i][0] + from_down[i][0] for i in range(2)]
            field = [
                [field[i][c] + from_up[i][1 + c] + from_down[i][1 + c] for c in range(3)]
                for i in range(2)
            ]
            inner = inner + from_up[0][5] + from_down[0][7]
            onward = [from_up[i][6:8] for i in range(2)]
            behind = [from_down[i][4:6] for i in range(2)]
        across = [[behind[i][j] + onward[i][j] for j in range(2)] for i in range(2)]
        rest = [ground[i] + (across[i][0] + across[i][1]) for i in range(2)]
        inv = block_inverse(rest, inner)
        solved = times(inv, [[ground[i]] + field[i] + [across[i][1]] for i in range(2)])
        other = times(across, [[after(x, 8) for x in line] for line in solved])
        ground = [ground[i] + other[i][0] for i in range(2)]
        field = [[field[i][c] + other[i][1 + c] for c in range(3)] for i in range(2)]
        inner = inner + other[0][4]
        value_c, value_d = times(block_inverse(ground, inner), field)
        value = {"c": value_c, "d": value_d}
        value["p"] = [before(x, 1) for x in value_c]
        value["q"] = [before(x, 1) for x in value_d]
        for (k, unused, ratio), y in zip(rsteps[::-1], rown[::-1]):
            value[k] = [summed([y[c]] + [r * value[a][c] for a, r in ratio.items()]) for c in range(3)]
        out = [value[n][c] for n in names for c in range(3)]
        for j, line in enumerate(out):
            xret[pl.ds(j, 16, stride=16), :] = line
        for k in (8, 7, 9, 5, 11, 4, 12, 3, 13, 6, 10, 2, 14, 1, 15):
            peer = lax.rem(gx + k, 16)
            push(2, xret, peer * 16, xback, chip * 16, 12, gx=peer)
        xback[pl.ds(pl.multiple_of(chip * 16, 8), 12), :] = xret[
            pl.ds(pl.multiple_of(gx * 16, 8), 12), :
        ]
        pl.semaphore_wait(far, 2)
        tell(wide, "gy", place(0, 1))
        tell(wide, "gy", place(0, -1))
        pl.semaphore_wait(wide, 2)
        tell(go, "gx", gx - 1)

    @pl.when(core == 0)
    def follow():
        pl.semaphore_wait(go, 1)

    exchange(1, cmsg, cin)

    @pl.when(core == 1)
    def seven():
        arrived(2, xback, 7 * 12)

    @pl.when(core == 0)
    def eight():
        arrived(2, xback, 8 * 12)

    got = [xback[pl.ds(j, 8, stride=16), :] for j in range(12)]
    value = {a: got[3 * i : 3 * i + 3] for i, a in enumerate(ends)}
    for i in range(16):
        for c in range(3):
            if i in ends:
                x = value[i][c]
            else:
                x = summed([xbase[i][c]] + [w * value[a][c] for a, w in xunit[i].items()])
            half[pl.ds(128 * c + 8 * i, 8), :] = x

    lines = [[half[pl.ds(128 * c + j, 16, stride=8), :] for c in range(3)] for j in range(8)]
    for i, end in enumerate((0, 7)):
        for c in range(3):
            ymsg[pl.ds(3 * i + c, 16, stride=8), :] = summed(
                [lines[end][c]] + [yunit[k][end] * lines[k][c] for k in range(1, 7) if end in yunit[k]]
            )
    exchange(3, ymsg, yin)
    source = {j: list(lines[j]) for j in range(8)}
    yown = [forward(step, source) for step in ysteps]
    ybase, unused = responses(ysteps, yown, (0, 7))

    arrived(1, cin, 15 * 8)
    link, ground_a, ground_b, eta0, eta7 = [cin[pl.ds(j, 16, stride=8), :] for j in range(5)]
    segment = lax.broadcasted_iota(jnp.int32, (16, 128), 0)

    def lower(x, h):
        return pltpu.roll(x, h, 0)

    def upper(x, h):
        return pltpu.roll(x, 16 - h, 0)

    gate = jnp.where(segment == 0, 0.0, lower(eta7, 1) + eta0)
    inverse_a = 1.0 / (ground_a + link + gate)
    to_b, to_q = link * inverse_a, gate * inverse_a
    low = to_q * link
    high = jnp.where(segment == 15, 0.0, upper(low, 1))
    to_b_up = jnp.where(segment == 15, 0.0, upper(to_q, 1))
    ground = ground_b + to_b * ground_a + to_b_up * upper(ground_a, 1)
    sweeps = []
    for h in (1, 2, 4, 8):
        inverse = 1.0 / (ground + low + high)
        weight_low, weight_high = low * lower(inverse, h), high * upper(inverse, h)
        sweeps.append((h, weight_low, weight_high))
        ground = ground + weight_low * lower(ground, h) + weight_high * upper(ground, h)
        low, high = weight_low * lower(low, h), weight_high * upper(high, h)
    inverse_b = 1.0 / ground

    arrived(3, yin, 15 * 8)
    ends_a = [yin[pl.ds(c, 16, stride=8), :] for c in range(3)]
    ends_b = [yin[pl.ds(3 + c, 16, stride=8), :] for c in range(3)]
    for c in range(3):
        f = ends_b[c] + to_b * ends_a[c] + to_b_up * upper(ends_a[c], 1)
        for h, weight_low, weight_high in sweeps:
            f = f + weight_low * lower(f, h) + weight_high * upper(f, h)
        f = f * inverse_b
        yret[pl.ds(3 + c, 16, stride=8), :] = f
        yret[pl.ds(c, 16, stride=8), :] = inverse_a * ends_a[c] + to_b * f + to_q * lower(f, 1)
    exchange(4, yret, yback)

    arrived(4, yback, 15 * 8)
    first = [yback[pl.ds(c, 16, stride=8), :] for c in range(3)]
    final = [yback[pl.ds(3 + c, 16, stride=8), :] for c in range(3)]
    for c in range(3):
        for j in range(8):
            if j == 0:
                x = first[c]
            elif j == 7:
                x = final[c]
            else:
                x = ybase[j][c] + (yunit[j][0] * first[c] + yunit[j][7] * final[c])
            adv[pl.ds(128 * c + j, 16, stride=8), :] = x

    departed(0, xmsg, 7 * 26)
    departed(1, cmsg, 15 * 8)
    departed(3, ymsg, 15 * 8)
    departed(4, yret, 15 * 8)

    @pl.when(core == 0)
    def lent():
        departed(0, xmsg, 26)

    @pl.when(core == 1)
    def returned():
        departed(2, xret, 15 * 12)


def store(half, adv, half_hbm, adv_hbm, done):
    copies = [
        pltpu.make_async_copy(half, half_hbm, done.at[0]),
        pltpu.make_async_copy(adv, adv_hbm, done.at[1]),
    ]
    for copy in copies:
        copy.start()
    for copy in copies:
        copy.wait()


def on_device(velocity, viscosity):
    vmem, hbm = pl.BlockSpec(memory_space=pltpu.VMEM), pl.BlockSpec(memory_space=pltpu.HBM)
    small, large = pltpu.VMEM((128, 128), F32), pltpu.VMEM((256, 128), F32)
    huge = pltpu.VMEM((512, 128), F32)
    held = [
        pltpu.with_memory_space_constraint(x, pltpu.HBM)
        for x in (velocity.reshape(384, 128), viscosity.reshape(128, 128))
    ]
    half, adv = pl.pallas_call(
        kernel,
        name="adi",
        out_shape=[jax.ShapeDtypeStruct((384, 128), F32)] * 2,
        in_specs=[hbm, hbm],
        out_specs=[vmem, vmem],
        scratch_shapes=[pltpu.VMEM((384, 128), F32), small, pltpu.SemaphoreType.DMA((2,)), large, huge, large] + [small] * 7
        + [pltpu.SemaphoreType.DMA((5,)), pltpu.SemaphoreType.DMA((5,))]
        + [pltpu.SemaphoreType.REGULAR] * 4,
        compiler_params=pltpu.CompilerParams(
            collective_id=0, has_side_effects=True, vmem_limit_bytes=32 * 1024 * 1024
        ),
    )(*held)
    half, adv = pl.pallas_call(
        store,
        name="store",
        out_shape=[jax.ShapeDtypeStruct((384, 128), F32)] * 2,
        in_specs=[vmem, vmem],
        out_specs=[hbm, hbm],
        scratch_shapes=[pltpu.SemaphoreType.DMA((2,))],
        compiler_params=pltpu.CompilerParams(vmem_limit_bytes=1024 * 1024),
    )(half, adv)
    return half.reshape(velocity.shape), adv.reshape(velocity.shape)


def solution(mesh):
    return jax.shard_map(
        on_device,
        mesh=mesh,
        in_specs=(P(None, "gx", "gy", None), P("gx", "gy", None)),
        out_specs=(P(None, "gx", "gy", None), P(None, "gx", "gy", None)),
        check_vma=False,
    )
```

```python
import jax
import jax.numpy as jnp
from jax import lax
from jax.experimental import pallas as pl
from jax.experimental.pallas import tpu as pltpu
from jax.sharding import PartitionSpec as P

MESH = pl.DeviceIdType.MESH
PLACES = (6, 7, 0, 1)
SOLVERS = tuple(8 * side + p for side in range(2) for p in PLACES)
F32 = jnp.float32


class Network:
    def __init__(self):
        self.edge = {}
        self.ground = {}

    def join(self, a, b, w):
        k = (a, b) if a < b else (b, a)
        self.edge[k] = self.edge[k] + w if k in self.edge else w

    def add_ground(self, a, w):
        self.ground[a] = self.ground[a] + w if a in self.ground else w

    def eliminate(self, k):
        near = {}
        for a, b in list(self.edge):
            if k in (a, b):
                near[b if a == k else a] = self.edge.pop((a, b))
        ground = self.ground.pop(k)
        total = ground
        for w in near.values():
            total = total + w
        inverse = 1.0 / total
        ratio = {a: w * inverse for a, w in near.items()}
        names = sorted(near)
        for i, a in enumerate(names):
            self.add_ground(a, ratio[a] * ground)
            for b in names[i + 1 :]:
                self.join(a, b, ratio[a] * near[b])
        return k, inverse, ratio


def forward(step, source):
    k, inverse, ratio = step
    here = source.pop(k)
    for a, r in ratio.items():
        part = [r * h for h in here]
        source[a] = [s + t for s, t in zip(source[a], part)] if a in source else part
    return [h * inverse for h in here]


def summed(values):
    values = list(values)
    while len(values) > 1:
        values = [
            values[i] + values[i + 1] if i + 1 < len(values) else values[i]
            for i in range(0, len(values), 2)
        ]
    return values[0]


def responses(steps, own, terminals):
    base, unit = {}, {}
    for (k, inverse, ratio), y in reversed(list(zip(steps, own))):
        inner = [(a, r) for a, r in ratio.items() if a not in terminals]
        if y is not None:
            base[k] = [
                summed([y[c]] + [r * base[a][c] for a, r in inner]) for c in range(len(y))
            ]
        unit[k] = {}
        for t in terminals:
            terms = [r * unit[a][t] for a, r in inner if t in unit[a]]
            if t in ratio:
                terms.append(ratio[t])
            if terms:
                unit[k][t] = summed(terms)
    return base, unit


def kernel(
    vel_hbm, visc_hbm, half, adv,
    vel, visc, load, xmsg, xin, xret, xback, cmsg, cin, ymsg, yin, yret, yback, send, recv, near, far, wide, go,
):
    gx, gy = lax.axis_index("gx"), lax.axis_index("gy")
    barrier = pltpu.get_barrier_semaphore()
    def place(side, move):
        return lax.rem(gy // 8 + side, 2) * 8 + lax.rem(gy + 8 + move, 8)

    def tell(semaphore, axis, peer):
        pl.semaphore_signal(semaphore, inc=1, device_id={axis: peer}, device_id_type=MESH)

    chip, core = gx // 2, lax.rem(gx, 2)

    around = (place(1, 1), place(1, -1), place(1, 0), place(0, 1), place(0, -1))

    @pl.when(core == 1)
    def announce():
        for peer in around:
            tell(barrier, "gy", peer)
        for k in (12, 4, 13, 11, 5, 3, 14, 10, 6, 2, 9, 7, 8, 1, 15):
            tell(barrier, "gx", lax.rem(gx + k, 16))

    @pl.when(core == 0)
    def report():
        tell(barrier, "gx", gx + 1)

    loads = [
        pltpu.make_async_copy(visc_hbm, visc, load.at[0]),
        pltpu.make_async_copy(vel_hbm, vel, load.at[1]),
    ]
    for copy in loads:
        copy.start()

    def push(index, source, start, target, to, rows, **place):
        pltpu.make_async_remote_copy(
            src_ref=source.at[pl.ds(start if isinstance(start, int) else pl.multiple_of(start, 8), rows)],
            dst_ref=target.at[pl.ds(pl.multiple_of(to, 8), rows)],
            send_sem=send.at[index],
            recv_sem=recv.at[index],
            device_id=place,
            device_id_type=MESH,
        ).start()

    spot = lax.rem(gy, 8)
    solves = (spot == PLACES[0]) | (spot == PLACES[1]) | (spot == PLACES[2]) | (spot == PLACES[3])
    rank = (gy // 8) * 4 + sum(i * (spot == p).astype(jnp.int32) for i, p in enumerate(PLACES))

    def stay(source, start, target, to, rows):
        target[pl.ds(pl.multiple_of(to, 8), rows), :] = source[
            pl.ds(pl.multiple_of(start, 8), rows), :
        ]

    def hand_in(index, source, target, rows):
        for at in (0, 4, 3, 7, 1, 5, 2, 6):

            @pl.when(gy != SOLVERS[at])
            def lend_row(at=at):
                push(index, source, 16 * at, target, gy * 16, rows, gy=SOLVERS[at])

        @pl.when(solves)
        def keep_row():
            stay(source, rank * 16, target, gy * 16, rows)

    def hand_back(index, source, target, rows):
        for at in (0, 8, 1, 9, 2, 10, 3, 11, 7, 15, 6, 14, 5, 13, 4, 12):

            @pl.when(gy != at)
            def return_row(at=at):
                push(index, source, 16 * at, target, rank * 16, rows, gy=at)

        stay(source, gy * 16, target, rank * 16, rows)

    def by_row(ref, name, rows, value=None):
        if value is None:
            return jnp.concatenate(
                [ref[pl.ds(rows * r + name, 8, stride=16), :] for r in range(2)], axis=0
            )
        for r in range(2):
            ref[pl.ds(rows * r + name, 8, stride=16), :] = value[8 * r : 8 * r + 8]

    def arrived(index, target, rows):
        some = target.at[pl.ds(0, rows)]
        pltpu.make_async_copy(some, some, recv.at[index]).wait()

    def departed(index, source, rows):
        some = source.at[pl.ds(0, rows)]
        pltpu.make_async_copy(some, some, send.at[index]).wait()

    for copy in loads:
        copy.wait()

    nu = [visc[pl.ds(8 * i, 8), :] for i in range(16)]
    net = Network()
    for i in range(16):
        net.add_ground(i, 1.0)
        if i < 15:
            net.join(i, i + 1, (nu[i] + nu[i + 1]) * 0.5)
        if i < 14:
            net.join(i, i + 2, (nu[i] + nu[i + 2]) * 0.125)
    source = {i: [vel[pl.ds(128 * c + 8 * i, 8), :] for c in range(3)] for i in range(16)}
    steps, own = [], []
    for k in (2, 13, 3, 12, 4, 11, 5, 10, 6, 9, 7, 8):
        step = net.eliminate(k)
        steps.append(step)
        own.append(forward(step, source))
    ends = (0, 1, 14, 15)
    out = [net.edge[e] for e in ((0, 1), (0, 14), (0, 15), (1, 14), (1, 15), (14, 15))]
    out += [net.ground[a] for a in ends] + [nu[a] for a in ends]
    out += [source[a][c] for a in ends for c in range(3)]
    for j, value in enumerate(out):
        xmsg[pl.ds(j, 8, stride=32), :] = value

    pl.semaphore_wait(barrier, 8 + 5 * core)
    for k in (4, 3, 5, 2, 6, 1, 7):
        peer = lax.rem(chip + k, 8)
        push(0, xmsg, peer * 32, xin, gx * 32, 26, gx=peer * 2 + 1)

    @pl.when(core == 0)
    def lend():
        push(0, xmsg, chip * 32, xin, gx * 32, 26, gx=gx + 1)

    @pl.when(core == 1)
    def keep():
        for peer in around:
            tell(near, "gy", peer)
        xin[pl.ds(pl.multiple_of(gx * 32, 8), 26), :] = xmsg[
            pl.ds(pl.multiple_of(chip * 32, 8), 26), :
        ]

    eta = [visc[pl.ds(j, 16, stride=8), :] for j in range(8)]
    net = Network()
    for j in range(8):
        net.add_ground(j, 1.0)
        if j < 7:
            net.join(j, j + 1, eta[j] + eta[j + 1])
    net.add_ground(0, eta[0] * (gy == 0).astype(F32))
    net.add_ground(7, eta[7] * (gy == 15).astype(F32))
    ysteps = [net.eliminate(k) for k in (1, 6, 2, 5, 3, 4)]
    for j, value in enumerate((net.edge[(0, 7)], net.ground[0], net.ground[7], eta[0], eta[7])):
        by_row(cmsg, j, 5, value)

    xbase, xunit = responses(steps, own, ends)
    unused, yunit = responses(ysteps, [None] * 6, (0, 7))

    @pl.when(core == 1)
    def solve_ring():
        pl.semaphore_wait(near, 5)
        tell(far, "gy", place(0, 2))
        tell(far, "gy", place(0, -2))

        arrived(0, xin, 15 * 26)
        got = [xin[pl.ds(j, 16, stride=32), :] for j in range(26)]
        ring = Network()
        names = ("a", "b", "c", "d")
        for e, (i, j) in enumerate(((0, 1), (0, 2), (0, 3), (1, 2), (1, 3), (2, 3))):
            ring.join(names[i], names[j], got[e])
        for i in range(4):
            ring.add_ground(names[i], got[6 + i])
        rhs = {names[i]: got[14 + 3 * i : 17 + 3 * i] for i in range(4)}
        nu0, nu1, nu14, nu15 = got[10:14]

        def after(x, h):
            return pltpu.roll(x, 16 - h, 0)

        def before(x, h):
            return pltpu.roll(x, h, 0)

        last14, last15 = before(nu14, 1), before(nu15, 1)
        ring.join("a", "q", (last15 + nu0) * 0.5)
        ring.join("a", "p", (last14 + nu0) * 0.125)
        ring.join("b", "q", (last15 + nu1) * 0.125)
        rsteps = [ring.eliminate("a")]
        rown = [forward(rsteps[0], rhs)]
        rsteps.append(ring.eliminate("b"))
        rown.append(forward(rsteps[1], rhs))
        behind = [[ring.edge[("c", "p")], ring.edge[("c", "q")]], [ring.edge[("d", "p")], ring.edge[("d", "q")]]]
        onward = [[after(behind[j][i], 1) for j in range(2)] for i in range(2)]
        ground = [ring.ground["c"] + after(ring.ground["p"], 1), ring.ground["d"] + after(ring.ground["q"], 1)]
        inner = ring.edge[("c", "d")] + after(ring.edge[("p", "q")], 1)
        field = [
            [rhs[n][c] + after(rhs[m][c], 1) for c in range(3)] for n, m in (("c", "p"), ("d", "q"))
        ]

        def block_inverse(rest, link):
            scale = 1.0 / (rest[0] * rest[1] + link * (rest[0] + rest[1]))
            cross = link * scale
            return [[rest[1] * scale + cross, cross], [cross, rest[0] * scale + cross]]

        def times(m, v):
            return [[m[i][0] * v[0][j] + m[i][1] * v[1][j] for j in range(len(v[0]))] for i in range(2)]

        for h in (1, 2, 4):
            rest = [
                ground[i] + ((behind[i][0] + behind[i][1]) + (onward[i][0] + onward[i][1]))
                for i in range(2)
            ]
            inv = block_inverse(rest, inner)
            solved = times(inv, [[ground[i]] + field[i] + behind[i] + onward[i] for i in range(2)])
            up = [[after(x, h) for x in line] for line in solved]
            down = [[before(x, h) for x in line] for line in solved]
            from_up, from_down = times(onward, up), times(behind, down)
            ground = [ground[i] + from_up[i][0] + from_down[i][0] for i in range(2)]
            field = [
                [field[i][c] + from_up[i][1 + c] + from_down[i][1 + c] for c in range(3)]
                for i in range(2)
            ]
            inner = inner + from_up[0][5] + from_down[0][7]
            onward = [from_up[i][6:8] for i in range(2)]
            behind = [from_down[i][4:6] for i in range(2)]
        across = [[behind[i][j] + onward[i][j] for j in range(2)] for i in range(2)]
        rest = [ground[i] + (across[i][0] + across[i][1]) for i in range(2)]
        inv = block_inverse(rest, inner)
        solved = times(inv, [[ground[i]] + field[i] + [across[i][1]] for i in range(2)])
        other = times(across, [[after(x, 8) for x in line] for line in solved])
        ground = [ground[i] + other[i][0] for i in range(2)]
        field = [[field[i][c] + other[i][1 + c] for c in range(3)] for i in range(2)]
        inner = inner + other[0][4]
        value_c, value_d = times(block_inverse(ground, inner), field)
        value = {"c": value_c, "d": value_d}
        value["p"] = [before(x, 1) for x in value_c]
        value["q"] = [before(x, 1) for x in value_d]
        for (k, unused, ratio), y in zip(rsteps[::-1], rown[::-1]):
            value[k] = [summed([y[c]] + [r * value[a][c] for a, r in ratio.items()]) for c in range(3)]
        out = [value[n][c] for n in names for c in range(3)]
        for j, line in enumerate(out):
            xret[pl.ds(j, 16, stride=16), :] = line
        for k in (8, 7, 9, 5, 11, 4, 12, 3, 13, 6, 10, 2, 14, 1, 15):
            peer = lax.rem(gx + k, 16)
            push(2, xret, peer * 16, xback, chip * 16, 12, gx=peer)
        xback[pl.ds(pl.multiple_of(chip * 16, 8), 12), :] = xret[
            pl.ds(pl.multiple_of(gx * 16, 8), 12), :
        ]
        pl.semaphore_wait(far, 2)
        tell(wide, "gy", place(0, 1))
        tell(wide, "gy", place(0, -1))
        pl.semaphore_wait(wide, 2)
        tell(go, "gx", gx - 1)

    @pl.when(core == 0)
    def follow():
        pl.semaphore_wait(go, 1)

    hand_in(1, cmsg, cin, 10)

    @pl.when(core == 1)
    def seven():
        arrived(2, xback, 7 * 12)

    @pl.when(core == 0)
    def eight():
        arrived(2, xback, 8 * 12)

    got = [xback[pl.ds(j, 8, stride=16), :] for j in range(12)]
    value = {a: got[3 * i : 3 * i + 3] for i, a in enumerate(ends)}
    for i in range(16):
        for c in range(3):
            if i in ends:
                x = value[i][c]
            else:
                x = summed([xbase[i][c]] + [w * value[a][c] for a, w in xunit[i].items()])
            half[pl.ds(128 * c + 8 * i, 8), :] = x

    lines = [[half[pl.ds(128 * c + j, 16, stride=8), :] for c in range(3)] for j in range(8)]
    for i, end in enumerate((0, 7)):
        for c in range(3):
            value = summed(
                [lines[end][c]] + [yunit[k][end] * lines[k][c] for k in range(1, 7) if end in yunit[k]]
            )
            by_row(ymsg, 3 * i + c, 6, value)
    hand_in(3, ymsg, yin, 12)
    source = {j: list(lines[j]) for j in range(8)}
    yown = [forward(step, source) for step in ysteps]
    ybase, unused = responses(ysteps, yown, (0, 7))

    segment = lax.broadcasted_iota(jnp.int32, (16, 128), 0)

    def lower(x, h):
        return pltpu.roll(x, h, 0)

    def upper(x, h):
        return pltpu.roll(x, 16 - h, 0)

    def factor(r):
        link, ground_a, ground_b, eta0, eta7 = [
            cin[pl.ds(5 * r + j, 16, stride=16), :] for j in range(5)
        ]
        gate = jnp.where(segment == 0, 0.0, lower(eta7, 1) + eta0)
        inverse_a = 1.0 / (ground_a + link + gate)
        to_b, to_q = link * inverse_a, gate * inverse_a
        low = to_q * link
        high = jnp.where(segment == 15, 0.0, upper(low, 1))
        to_b_up = jnp.where(segment == 15, 0.0, upper(to_q, 1))
        ground = ground_b + to_b * ground_a + to_b_up * upper(ground_a, 1)
        sweeps = []
        for h in (1, 2, 4, 8):
            inverse = 1.0 / (ground + low + high)
            weight_low, weight_high = low * lower(inverse, h), high * upper(inverse, h)
            sweeps.append((h, weight_low, weight_high))
            ground = ground + weight_low * lower(ground, h) + weight_high * upper(ground, h)
            low, high = weight_low * lower(low, h), weight_high * upper(high, h)
        return inverse_a, to_b, to_q, to_b_up, sweeps, 1.0 / ground

    def solve_row(r, factors):
        inverse_a, to_b, to_q, to_b_up, sweeps, inverse_b = factors
        for c in range(3):
            end_a = yin[pl.ds(6 * r + c, 16, stride=16), :]
            f = yin[pl.ds(6 * r + 3 + c, 16, stride=16), :]
            f = f + to_b * end_a + to_b_up * upper(end_a, 1)
            for h, weight_low, weight_high in sweeps:
                f = f + weight_low * lower(f, h) + weight_high * upper(f, h)
            f = f * inverse_b
            yret[pl.ds(6 * r + 3 + c, 16, stride=16), :] = f
            yret[pl.ds(6 * r + c, 16, stride=16), :] = (
                inverse_a * end_a + to_b * f + to_q * lower(f, 1)
            )

    @pl.when(solves)
    def solve_rows():
        arrived(1, cin, 15 * 10)
        factors = [factor(r) for r in range(2)]
        arrived(3, yin, 15 * 12)
        for r in range(2):
            solve_row(r, factors[r])
        hand_back(4, yret, yback, 12)
        arrived(4, yback, 7 * 12)

    @pl.when(jnp.logical_not(solves))
    def await_rows():
        arrived(4, yback, 8 * 12)

    first = [by_row(yback, c, 6) for c in range(3)]
    final = [by_row(yback, 3 + c, 6) for c in range(3)]
    for c in range(3):
        for j in range(8):
            if j == 0:
                x = first[c]
            elif j == 7:
                x = final[c]
            else:
                x = ybase[j][c] + (yunit[j][0] * first[c] + yunit[j][7] * final[c])
            adv[pl.ds(128 * c + j, 16, stride=8), :] = x

    departed(0, xmsg, 7 * 26)
    departed(1, cmsg, 7 * 10)
    departed(3, ymsg, 7 * 12)

    @pl.when(solves)
    def answered():
        departed(4, yret, 15 * 12)

    @pl.when(jnp.logical_not(solves))
    def asked():
        departed(1, cmsg, 10)
        departed(3, ymsg, 12)

    @pl.when(core == 0)
    def lent():
        departed(0, xmsg, 26)

    @pl.when(core == 1)
    def returned():
        departed(2, xret, 15 * 12)


def store(half, adv, half_hbm, adv_hbm, done):
    copies = [
        pltpu.make_async_copy(half, half_hbm, done.at[0]),
        pltpu.make_async_copy(adv, adv_hbm, done.at[1]),
    ]
    for copy in copies:
        copy.start()
    for copy in copies:
        copy.wait()


def on_device(velocity, viscosity):
    vmem, hbm = pl.BlockSpec(memory_space=pltpu.VMEM), pl.BlockSpec(memory_space=pltpu.HBM)
    small, large = pltpu.VMEM((128, 128), F32), pltpu.VMEM((256, 128), F32)
    huge = pltpu.VMEM((512, 128), F32)
    held = [
        pltpu.with_memory_space_constraint(x, pltpu.HBM)
        for x in (velocity.reshape(384, 128), viscosity.reshape(128, 128))
    ]
    half, adv = pl.pallas_call(
        kernel,
        name="adi",
        out_shape=[jax.ShapeDtypeStruct((384, 128), F32)] * 2,
        in_specs=[hbm, hbm],
        out_specs=[vmem, vmem],
        scratch_shapes=[pltpu.VMEM((384, 128), F32), small, pltpu.SemaphoreType.DMA((2,)), large, huge, large, small, small, large, small, large, large, small]
        + [pltpu.SemaphoreType.DMA((5,)), pltpu.SemaphoreType.DMA((5,))]
        + [pltpu.SemaphoreType.REGULAR] * 4,
        compiler_params=pltpu.CompilerParams(
            collective_id=0, has_side_effects=True, vmem_limit_bytes=32 * 1024 * 1024
        ),
    )(*held)
    half, adv = pl.pallas_call(
        store,
        name="store",
        out_shape=[jax.ShapeDtypeStruct((384, 128), F32)] * 2,
        in_specs=[vmem, vmem],
        out_specs=[hbm, hbm],
        scratch_shapes=[pltpu.SemaphoreType.DMA((2,))],
        compiler_params=pltpu.CompilerParams(vmem_limit_bytes=1024 * 1024),
    )(half, adv)
    return half.reshape(velocity.shape), adv.reshape(velocity.shape)


def solution(mesh):
    return jax.shard_map(
        on_device,
        mesh=mesh,
        in_specs=(P(None, "gx", "gy", None), P("gx", "gy", None)),
        out_specs=(P(None, "gx", "gy", None), P(None, "gx", "gy", None)),
        check_vma=False,
    )
```

```python
import jax
import jax.numpy as jnp
from jax import lax
from jax.experimental import pallas as pl
from jax.experimental.pallas import tpu as pltpu
from jax.sharding import PartitionSpec as P

MESH = pl.DeviceIdType.MESH
F32 = jnp.float32
ORDER = (0, 4, 3, 7, 1, 5, 2, 6)
BACK = (0, 8, 1, 9, 2, 10, 3, 11, 7, 15, 6, 14, 5, 13, 4, 12)


class Network:
    def __init__(self):
        self.edge = {}
        self.ground = {}

    def join(self, a, b, w):
        k = (a, b) if a < b else (b, a)
        self.edge[k] = self.edge[k] + w if k in self.edge else w

    def add_ground(self, a, w):
        self.ground[a] = self.ground[a] + w if a in self.ground else w

    def eliminate(self, k):
        near = {}
        for a, b in list(self.edge):
            if k in (a, b):
                near[b if a == k else a] = self.edge.pop((a, b))
        ground = self.ground.pop(k)
        total = ground
        for w in near.values():
            total = total + w
        inverse = 1.0 / total
        ratio = {a: w * inverse for a, w in near.items()}
        names = sorted(near)
        for i, a in enumerate(names):
            self.add_ground(a, ratio[a] * ground)
            for b in names[i + 1 :]:
                self.join(a, b, ratio[a] * near[b])
        return k, inverse, ratio


def forward(step, source):
    k, inverse, ratio = step
    here = source.pop(k)
    for a, r in ratio.items():
        part = [r * h for h in here]
        source[a] = [s + t for s, t in zip(source[a], part)] if a in source else part
    return [h * inverse for h in here]


def summed(values):
    values = list(values)
    while len(values) > 1:
        values = [
            values[i] + values[i + 1] if i + 1 < len(values) else values[i]
            for i in range(0, len(values), 2)
        ]
    return values[0]


def responses(steps, own, terminals):
    base, unit = {}, {}
    for (k, inverse, ratio), y in reversed(list(zip(steps, own))):
        inner = [(a, r) for a, r in ratio.items() if a not in terminals]
        if y is not None:
            base[k] = [
                summed([y[c]] + [r * base[a][c] for a, r in inner]) for c in range(len(y))
            ]
        unit[k] = {}
        for t in terminals:
            terms = [r * unit[a][t] for a, r in inner if t in unit[a]]
            if t in ratio:
                terms.append(ratio[t])
            if terms:
                unit[k][t] = summed(terms)
    return base, unit


def kernel(
    vel_hbm, visc_hbm, half, adv,
    vel, visc, load, xmsg, xin, xret, xback, cmsg, cin, ymsg, yin, yret, yback, send, recv, near, far, go,
):
    gx, gy = lax.axis_index("gx"), lax.axis_index("gy")
    barrier = pltpu.get_barrier_semaphore()
    def place(side, move):
        return lax.rem(gy // 8 + side, 2) * 8 + lax.rem(gy + 8 + move, 8)

    def tell(semaphore, axis, peer):
        pl.semaphore_signal(semaphore, inc=1, device_id={axis: peer}, device_id_type=MESH)

    chip, core = gx // 2, lax.rem(gx, 2)

    around = (place(1, 1), place(1, -1), place(1, 0), place(0, 1), place(0, -1))

    @pl.when(core == 1)
    def announce():
        for peer in around:
            tell(barrier, "gy", peer)
        for k in (12, 4, 13, 11, 5, 3, 14, 10, 6, 2, 9, 7, 8, 1, 15):
            tell(barrier, "gx", lax.rem(gx + k, 16))

    loads = [
        pltpu.make_async_copy(visc_hbm, visc, load.at[0]),
        pltpu.make_async_copy(vel_hbm, vel, load.at[1]),
    ]
    for copy in loads:
        copy.start()

    def push(index, source, start, target, to, rows, **place):
        pltpu.make_async_remote_copy(
            src_ref=source.at[pl.ds(start if isinstance(start, int) else pl.multiple_of(start, 8), rows)],
            dst_ref=target.at[pl.ds(pl.multiple_of(to, 8), rows)],
            send_sem=send.at[index],
            recv_sem=recv.at[index],
            device_id=place,
            device_id_type=MESH,
        ).start()

    spot = lax.rem(gy, 8)
    swap = (chip == 0).astype(jnp.int32)
    upper_first, upper_second = swap, 1 - swap
    own_rows = (spot // 4 == upper_second).astype(jnp.int32)
    rank = (gy // 8) * 4 + lax.rem(spot, 4)

    def solver(at, upper):
        return (at // 4) * 8 + at % 4 + 4 * upper

    def stay(source, start, target, to, rows):
        target[pl.ds(pl.multiple_of(to, 8), rows), :] = source[
            pl.ds(pl.multiple_of(start, 8), rows), :
        ]

    def hand_in(index, source, target, rows):
        @pl.when(core == 0)
        def lend_rows():
            for at in ORDER:
                push(index, source, 16 * at, target, gy * 16, rows, gx=gx + 1, gy=solver(at, upper_first))

        @pl.when(core == 1)
        def give_rows():
            for at in ORDER:

                @pl.when(gy != solver(at, upper_second))
                def give_row(at=at):
                    push(index, source, 16 * at, target, gy * 16, rows, gx=gx, gy=solver(at, upper_second))

            @pl.when(own_rows == 1)
            def keep_row():
                stay(source, rank * 16, target, gy * 16, rows)

    def hand_back(index, source, target, rows):
        @pl.when(own_rows == 0)
        def return_rows():
            for at in BACK:
                push(index, source, 16 * at, target, rank * 16, rows, gx=gx - 1, gy=at)

        @pl.when(own_rows == 1)
        def pass_rows():
            for at in BACK:

                @pl.when(gy != at)
                def pass_row(at=at):
                    push(index, source, 16 * at, target, rank * 16, rows, gx=gx, gy=at)

            stay(source, gy * 16, target, rank * 16, rows)

    def by_row(ref, name, rows, value=None):
        if value is None:
            return jnp.concatenate(
                [ref[pl.ds(rows * r + name, 8, stride=16), :] for r in range(2)], axis=0
            )
        for r in range(2):
            ref[pl.ds(rows * r + name, 8, stride=16), :] = value[8 * r : 8 * r + 8]

    def arrived(index, target, rows):
        some = target.at[pl.ds(0, rows)]
        pltpu.make_async_copy(some, some, recv.at[index]).wait()

    def departed(index, source, rows):
        some = source.at[pl.ds(0, rows)]
        pltpu.make_async_copy(some, some, send.at[index]).wait()

    for copy in loads:
        copy.wait()

    nu = [visc[pl.ds(8 * i, 8), :] for i in range(16)]
    net = Network()
    for i in range(16):
        net.add_ground(i, 1.0)
        if i < 15:
            net.join(i, i + 1, (nu[i] + nu[i + 1]) * 0.5)
        if i < 14:
            net.join(i, i + 2, (nu[i] + nu[i + 2]) * 0.125)
    source = {i: [vel[pl.ds(128 * c + 8 * i, 8), :] for c in range(3)] for i in range(16)}
    steps, own = [], []
    for k in (2, 13, 3, 12, 4, 11, 5, 10, 6, 9, 7, 8):
        step = net.eliminate(k)
        steps.append(step)
        own.append(forward(step, source))
    ends = (0, 1, 14, 15)
    out = [net.edge[e] for e in ((0, 1), (0, 14), (0, 15), (1, 14), (1, 15), (14, 15))]
    out += [net.ground[a] for a in ends] + [nu[a] for a in ends]
    out += [source[a][c] for a in ends for c in range(3)]
    for j, value in enumerate(out):
        xmsg[pl.ds(j, 8, stride=32), :] = value

    pl.semaphore_wait(barrier, 8 + 4 * core)
    for k in (4, 3, 5, 2, 6, 1, 7):
        peer = lax.rem(chip + k, 8)
        push(0, xmsg, peer * 32, xin, gx * 32, 26, gx=peer * 2 + 1)

    @pl.when(core == 0)
    def lend():
        push(0, xmsg, chip * 32, xin, gx * 32, 26, gx=gx + 1)

    @pl.when(core == 1)
    def keep():
        tell(near, "gy", place(0, 1))
        tell(near, "gy", place(0, -1))
        xin[pl.ds(pl.multiple_of(gx * 32, 8), 26), :] = xmsg[
            pl.ds(pl.multiple_of(chip * 32, 8), 26), :
        ]

    eta = [visc[pl.ds(j, 16, stride=8), :] for j in range(8)]
    net = Network()
    for j in range(8):
        net.add_ground(j, 1.0)
        if j < 7:
            net.join(j, j + 1, eta[j] + eta[j + 1])
    net.add_ground(0, eta[0] * (gy == 0).astype(F32))
    net.add_ground(7, eta[7] * (gy == 15).astype(F32))
    ysteps = [net.eliminate(k) for k in (1, 6, 2, 5, 3, 4)]
    for j, value in enumerate((net.edge[(0, 7)], net.ground[0], net.ground[7], eta[0], eta[7])):
        by_row(cmsg, j, 5, value)

    xbase, xunit = responses(steps, own, ends)
    unused, yunit = responses(ysteps, [None] * 6, (0, 7))

    @pl.when(core == 1)
    def solve_ring():
        pl.semaphore_wait(near, 2)
        tell(far, "gy", place(0, 2))
        tell(far, "gy", place(0, -2))

        arrived(0, xin, 15 * 26)
        got = [xin[pl.ds(j, 16, stride=32), :] for j in range(26)]
        ring = Network()
        names = ("a", "b", "c", "d")
        for e, (i, j) in enumerate(((0, 1), (0, 2), (0, 3), (1, 2), (1, 3), (2, 3))):
            ring.join(names[i], names[j], got[e])
        for i in range(4):
            ring.add_ground(names[i], got[6 + i])
        rhs = {names[i]: got[14 + 3 * i : 17 + 3 * i] for i in range(4)}
        nu0, nu1, nu14, nu15 = got[10:14]

        def after(x, h):
            return pltpu.roll(x, 16 - h, 0)

        def before(x, h):
            return pltpu.roll(x, h, 0)

        last14, last15 = before(nu14, 1), before(nu15, 1)
        ring.join("a", "q", (last15 + nu0) * 0.5)
        ring.join("a", "p", (last14 + nu0) * 0.125)
        ring.join("b", "q", (last15 + nu1) * 0.125)
        rsteps = [ring.eliminate("a")]
        rown = [forward(rsteps[0], rhs)]
        rsteps.append(ring.eliminate("b"))
        rown.append(forward(rsteps[1], rhs))
        behind = [[ring.edge[("c", "p")], ring.edge[("c", "q")]], [ring.edge[("d", "p")], ring.edge[("d", "q")]]]
        onward = [[after(behind[j][i], 1) for j in range(2)] for i in range(2)]
        ground = [ring.ground["c"] + after(ring.ground["p"], 1), ring.ground["d"] + after(ring.ground["q"], 1)]
        inner = ring.edge[("c", "d")] + after(ring.edge[("p", "q")], 1)
        field = [
            [rhs[n][c] + after(rhs[m][c], 1) for c in range(3)] for n, m in (("c", "p"), ("d", "q"))
        ]

        def block_inverse(rest, link):
            scale = 1.0 / (rest[0] * rest[1] + link * (rest[0] + rest[1]))
            cross = link * scale
            return [[rest[1] * scale + cross, cross], [cross, rest[0] * scale + cross]]

        def times(m, v):
            return [[m[i][0] * v[0][j] + m[i][1] * v[1][j] for j in range(len(v[0]))] for i in range(2)]

        for h in (1, 2, 4):
            rest = [
                ground[i] + ((behind[i][0] + behind[i][1]) + (onward[i][0] + onward[i][1]))
                for i in range(2)
            ]
            inv = block_inverse(rest, inner)
            solved = times(inv, [[ground[i]] + field[i] + behind[i] + onward[i] for i in range(2)])
            up = [[after(x, h) for x in line] for line in solved]
            down = [[before(x, h) for x in line] for line in solved]
            from_up, from_down = times(onward, up), times(behind, down)
            ground = [ground[i] + from_up[i][0] + from_down[i][0] for i in range(2)]
            field = [
                [field[i][c] + from_up[i][1 + c] + from_down[i][1 + c] for c in range(3)]
                for i in range(2)
            ]
            inner = inner + from_up[0][5] + from_down[0][7]
            onward = [from_up[i][6:8] for i in range(2)]
            behind = [from_down[i][4:6] for i in range(2)]
        across = [[behind[i][j] + onward[i][j] for j in range(2)] for i in range(2)]
        rest = [ground[i] + (across[i][0] + across[i][1]) for i in range(2)]
        inv = block_inverse(rest, inner)
        solved = times(inv, [[ground[i]] + field[i] + [across[i][1]] for i in range(2)])
        other = times(across, [[after(x, 8) for x in line] for line in solved])
        ground = [ground[i] + other[i][0] for i in range(2)]
        field = [[field[i][c] + other[i][1 + c] for c in range(3)] for i in range(2)]
        inner = inner + other[0][4]
        value_c, value_d = times(block_inverse(ground, inner), field)
        value = {"c": value_c, "d": value_d}
        value["p"] = [before(x, 1) for x in value_c]
        value["q"] = [before(x, 1) for x in value_d]
        for (k, unused, ratio), y in zip(rsteps[::-1], rown[::-1]):
            value[k] = [summed([y[c]] + [r * value[a][c] for a, r in ratio.items()]) for c in range(3)]
        out = [value[n][c] for n in names for c in range(3)]
        for j, line in enumerate(out):
            xret[pl.ds(j, 16, stride=16), :] = line
        for k in (8, 7, 9, 5, 11, 4, 12, 3, 13, 6, 10, 2, 14, 1, 15):
            peer = lax.rem(gx + k, 16)
            push(2, xret, peer * 16, xback, chip * 16, 12, gx=peer)
        xback[pl.ds(pl.multiple_of(chip * 16, 8), 12), :] = xret[
            pl.ds(pl.multiple_of(gx * 16, 8), 12), :
        ]
        pl.semaphore_wait(far, 2)
        tell(go, "gx", gx - 1)

    @pl.when(core == 0)
    def follow():
        pl.semaphore_wait(go, 1)

    hand_in(1, cmsg, cin, 10)

    @pl.when(core == 1)
    def seven():
        arrived(2, xback, 7 * 12)

    @pl.when(core == 0)
    def eight():
        arrived(2, xback, 8 * 12)

    got = [xback[pl.ds(j, 8, stride=16), :] for j in range(12)]
    value = {a: got[3 * i : 3 * i + 3] for i, a in enumerate(ends)}
    for i in range(16):
        for c in range(3):
            if i in ends:
                x = value[i][c]
            else:
                x = summed([xbase[i][c]] + [w * value[a][c] for a, w in xunit[i].items()])
            half[pl.ds(128 * c + 8 * i, 8), :] = x

    lines = [[half[pl.ds(128 * c + j, 16, stride=8), :] for c in range(3)] for j in range(8)]
    for i, end in enumerate((0, 7)):
        for c in range(3):
            value = summed(
                [lines[end][c]] + [yunit[k][end] * lines[k][c] for k in range(1, 7) if end in yunit[k]]
            )
            by_row(ymsg, 3 * i + c, 6, value)
    hand_in(3, ymsg, yin, 12)
    source = {j: list(lines[j]) for j in range(8)}
    yown = [forward(step, source) for step in ysteps]
    ybase, unused = responses(ysteps, yown, (0, 7))

    segment = lax.broadcasted_iota(jnp.int32, (16, 128), 0)

    def lower(x, h):
        return pltpu.roll(x, h, 0)

    def upper(x, h):
        return pltpu.roll(x, 16 - h, 0)

    def factor(r):
        link, ground_a, ground_b, eta0, eta7 = [
            cin[pl.ds(5 * r + j, 16, stride=16), :] for j in range(5)
        ]
        gate = jnp.where(segment == 0, 0.0, lower(eta7, 1) + eta0)
        inverse_a = 1.0 / (ground_a + link + gate)
        to_b, to_q = link * inverse_a, gate * inverse_a
        low = to_q * link
        high = jnp.where(segment == 15, 0.0, upper(low, 1))
        to_b_up = jnp.where(segment == 15, 0.0, upper(to_q, 1))
        ground = ground_b + to_b * ground_a + to_b_up * upper(ground_a, 1)
        sweeps = []
        for h in (1, 2, 4, 8):
            inverse = 1.0 / (ground + low + high)
            weight_low, weight_high = low * lower(inverse, h), high * upper(inverse, h)
            sweeps.append((h, weight_low, weight_high))
            ground = ground + weight_low * lower(ground, h) + weight_high * upper(ground, h)
            low, high = weight_low * lower(low, h), weight_high * upper(high, h)
        return inverse_a, to_b, to_q, to_b_up, sweeps, 1.0 / ground

    def solve_row(r, factors):
        inverse_a, to_b, to_q, to_b_up, sweeps, inverse_b = factors
        for c in range(3):
            end_a = yin[pl.ds(6 * r + c, 16, stride=16), :]
            f = yin[pl.ds(6 * r + 3 + c, 16, stride=16), :]
            f = f + to_b * end_a + to_b_up * upper(end_a, 1)
            for h, weight_low, weight_high in sweeps:
                f = f + weight_low * lower(f, h) + weight_high * upper(f, h)
            f = f * inverse_b
            yret[pl.ds(6 * r + 3 + c, 16, stride=16), :] = f
            yret[pl.ds(6 * r + c, 16, stride=16), :] = (
                inverse_a * end_a + to_b * f + to_q * lower(f, 1)
            )

    def arrived_or(index, target, rows, count):
        @pl.when(own_rows == 1)
        def but_own():
            arrived(index, target, (count - 1) * rows)

        @pl.when(own_rows == 0)
        def with_all():
            arrived(index, target, count * rows)

    @pl.when(core == 1)
    def solve_rows():
        arrived_or(1, cin, 10, 16)
        factors = [factor(r) for r in range(2)]
        arrived_or(3, yin, 12, 16)
        for r in range(2):
            solve_row(r, factors[r])
        hand_back(4, yret, yback, 12)
        arrived_or(4, yback, 12, 8)

    @pl.when(core == 0)
    def await_rows():
        arrived(4, yback, 8 * 12)

    first = [by_row(yback, c, 6) for c in range(3)]
    final = [by_row(yback, 3 + c, 6) for c in range(3)]
    for c in range(3):
        for j in range(8):
            if j == 0:
                x = first[c]
            elif j == 7:
                x = final[c]
            else:
                x = ybase[j][c] + (yunit[j][0] * first[c] + yunit[j][7] * final[c])
            adv[pl.ds(128 * c + j, 16, stride=8), :] = x

    departed(0, xmsg, 7 * 26)
    departed(1, cmsg, 7 * 10)
    departed(3, ymsg, 7 * 12)

    @pl.when(core == 0)
    def lent():
        departed(0, xmsg, 26)
        departed(1, cmsg, 10)
        departed(3, ymsg, 12)

    @pl.when(core == 1)
    def returned():
        departed(2, xret, 15 * 12)
        departed(4, yret, 15 * 12)

        @pl.when(own_rows == 0)
        def all_returned():
            departed(1, cmsg, 10)
            departed(3, ymsg, 12)
            departed(4, yret, 12)


def store(half, adv, half_hbm, adv_hbm, done):
    copies = [
        pltpu.make_async_copy(half, half_hbm, done.at[0]),
        pltpu.make_async_copy(adv, adv_hbm, done.at[1]),
    ]
    for copy in copies:
        copy.start()
    for copy in copies:
        copy.wait()


def on_device(velocity, viscosity):
    vmem, hbm = pl.BlockSpec(memory_space=pltpu.VMEM), pl.BlockSpec(memory_space=pltpu.HBM)
    small, large = pltpu.VMEM((128, 128), F32), pltpu.VMEM((256, 128), F32)
    huge = pltpu.VMEM((512, 128), F32)
    held = [
        pltpu.with_memory_space_constraint(x, pltpu.HBM)
        for x in (velocity.reshape(384, 128), viscosity.reshape(128, 128))
    ]
    half, adv = pl.pallas_call(
        kernel,
        name="adi",
        out_shape=[jax.ShapeDtypeStruct((384, 128), F32)] * 2,
        in_specs=[hbm, hbm],
        out_specs=[vmem, vmem],
        scratch_shapes=[pltpu.VMEM((384, 128), F32), small, pltpu.SemaphoreType.DMA((2,)), large, huge, large, small, small, large, small, large, large, small]
        + [pltpu.SemaphoreType.DMA((5,)), pltpu.SemaphoreType.DMA((5,))]
        + [pltpu.SemaphoreType.REGULAR] * 3,
        compiler_params=pltpu.CompilerParams(
            collective_id=0, has_side_effects=True, vmem_limit_bytes=32 * 1024 * 1024
        ),
    )(*held)
    half, adv = pl.pallas_call(
        store,
        name="store",
        out_shape=[jax.ShapeDtypeStruct((384, 128), F32)] * 2,
        in_specs=[vmem, vmem],
        out_specs=[hbm, hbm],
        scratch_shapes=[pltpu.SemaphoreType.DMA((2,))],
        compiler_params=pltpu.CompilerParams(vmem_limit_bytes=1024 * 1024),
    )(half, adv)
    return half.reshape(velocity.shape), adv.reshape(velocity.shape)


def solution(mesh):
    return jax.shard_map(
        on_device,
        mesh=mesh,
        in_specs=(P(None, "gx", "gy", None), P("gx", "gy", None)),
        out_specs=(P(None, "gx", "gy", None), P(None, "gx", "gy", None)),
        check_vma=False,
    )
```

```python
import jax
import jax.numpy as jnp
from jax import lax
from jax.experimental import pallas as pl
from jax.experimental.pallas import tpu as pltpu
from jax.sharding import PartitionSpec as P

MESH = pl.DeviceIdType.MESH
F32 = jnp.float32
ORDER = (0, 4, 3, 7, 1, 5, 2, 6)
BACK = (0, 8, 1, 9, 2, 10, 3, 11, 7, 15, 6, 14, 5, 13, 4, 12)


class Network:
    def __init__(self):
        self.edge = {}
        self.ground = {}

    def join(self, a, b, w):
        k = (a, b) if a < b else (b, a)
        self.edge[k] = self.edge[k] + w if k in self.edge else w

    def add_ground(self, a, w):
        self.ground[a] = self.ground[a] + w if a in self.ground else w

    def eliminate(self, k):
        near = {}
        for a, b in list(self.edge):
            if k in (a, b):
                near[b if a == k else a] = self.edge.pop((a, b))
        ground = self.ground.pop(k)
        total = ground
        for w in near.values():
            total = total + w
        inverse = 1.0 / total
        ratio = {a: w * inverse for a, w in near.items()}
        names = sorted(near)
        for i, a in enumerate(names):
            self.add_ground(a, ratio[a] * ground)
            for b in names[i + 1 :]:
                self.join(a, b, ratio[a] * near[b])
        return k, inverse, ratio


def forward(step, source):
    k, inverse, ratio = step
    here = source.pop(k)
    for a, r in ratio.items():
        part = [r * h for h in here]
        source[a] = [s + t for s, t in zip(source[a], part)] if a in source else part
    return [h * inverse for h in here]


def summed(values):
    values = list(values)
    while len(values) > 1:
        values = [
            values[i] + values[i + 1] if i + 1 < len(values) else values[i]
            for i in range(0, len(values), 2)
        ]
    return values[0]


def responses(steps, own, terminals):
    base, unit = {}, {}
    for (k, inverse, ratio), y in reversed(list(zip(steps, own))):
        inner = [(a, r) for a, r in ratio.items() if a not in terminals]
        if y is not None:
            base[k] = [
                summed([y[c]] + [r * base[a][c] for a, r in inner]) for c in range(len(y))
            ]
        unit[k] = {}
        for t in terminals:
            terms = [r * unit[a][t] for a, r in inner if t in unit[a]]
            if t in ratio:
                terms.append(ratio[t])
            if terms:
                unit[k][t] = summed(terms)
    return base, unit


def kernel(
    vel_hbm, visc_hbm, half, adv,
    vel, visc, load, xmsg, xin, xret, xback, cmsg, cin, ymsg, yin, yret, yback, send, recv, near, far, go,
):
    gx, gy = lax.axis_index("gx"), lax.axis_index("gy")
    barrier = pltpu.get_barrier_semaphore()
    def place(side, move):
        return lax.rem(gy // 8 + side, 2) * 8 + lax.rem(gy + 8 + move, 8)

    def tell(semaphore, axis, peer):
        pl.semaphore_signal(semaphore, inc=1, device_id={axis: peer}, device_id_type=MESH)

    chip, core = gx // 2, lax.rem(gx, 2)

    around = (place(1, 1), place(1, -1), place(1, 0), place(0, 1), place(0, -1))

    @pl.when(core == 1)
    def announce():
        for peer in around:
            tell(barrier, "gy", peer)
        for k in (12, 4, 13, 11, 5, 3, 14, 10, 6, 2, 9, 7, 8, 1, 15):
            tell(barrier, "gx", lax.rem(gx + k, 16))

    loads = [
        pltpu.make_async_copy(visc_hbm, visc, load.at[0]),
        pltpu.make_async_copy(vel_hbm, vel, load.at[1]),
    ]
    for copy in loads:
        copy.start()

    def push(index, source, start, target, to, rows, **place):
        pltpu.make_async_remote_copy(
            src_ref=source.at[pl.ds(start if isinstance(start, int) else pl.multiple_of(start, 8), rows)],
            dst_ref=target.at[pl.ds(pl.multiple_of(to, 8), rows)],
            send_sem=send.at[index],
            recv_sem=recv.at[index],
            device_id=place,
            device_id_type=MESH,
        ).start()

    spot = lax.rem(gy, 8)
    swap = (chip == 0).astype(jnp.int32)
    upper_first, upper_second = swap, 1 - swap
    own_rows = (spot // 4 == upper_second).astype(jnp.int32)
    rank = (gy // 8) * 4 + lax.rem(spot, 4)

    def solver(at, upper):
        return (at // 4) * 8 + at % 4 + 4 * upper

    def stay(source, start, target, to, rows):
        target[pl.ds(pl.multiple_of(to, 8), rows), :] = source[
            pl.ds(pl.multiple_of(start, 8), rows), :
        ]

    def hand_in(index, source, target, rows):
        @pl.when(core == 0)
        def lend_rows():
            for at in ORDER:
                push(index, source, 16 * at, target, gy * 16, rows, gx=gx + 1, gy=solver(at, upper_first))

        @pl.when(core == 1)
        def give_rows():
            for at in ORDER:

                @pl.when(gy != solver(at, upper_second))
                def give_row(at=at):
                    push(index, source, 16 * at, target, gy * 16, rows, gx=gx, gy=solver(at, upper_second))

            @pl.when(own_rows == 1)
            def keep_row():
                stay(source, rank * 16, target, gy * 16, rows)

    def hand_back(index, source, target, rows):
        @pl.when(own_rows == 0)
        def return_rows():
            for at in BACK:
                push(index, source, 16 * at, target, rank * 16, rows, gx=gx - 1, gy=at)

        @pl.when(own_rows == 1)
        def pass_rows():
            for at in BACK:

                @pl.when(gy != at)
                def pass_row(at=at):
                    push(index, source, 16 * at, target, rank * 16, rows, gx=gx, gy=at)

            stay(source, gy * 16, target, rank * 16, rows)

    def by_row(ref, name, rows, value=None):
        if value is None:
            return jnp.concatenate(
                [ref[pl.ds(rows * r + name, 8, stride=16), :] for r in range(2)], axis=0
            )
        for r in range(2):
            ref[pl.ds(rows * r + name, 8, stride=16), :] = value[8 * r : 8 * r + 8]

    def arrived(index, target, rows):
        some = target.at[pl.ds(0, rows)]
        pltpu.make_async_copy(some, some, recv.at[index]).wait()

    def departed(index, source, rows):
        some = source.at[pl.ds(0, rows)]
        pltpu.make_async_copy(some, some, send.at[index]).wait()

    for copy in loads:
        copy.wait()

    nu = [visc[pl.ds(8 * i, 8), :] for i in range(16)]
    net = Network()
    for i in range(16):
        net.add_ground(i, 1.0)
        if i < 15:
            net.join(i, i + 1, (nu[i] + nu[i + 1]) * 0.5)
        if i < 14:
            net.join(i, i + 2, (nu[i] + nu[i + 2]) * 0.125)
    source = {i: [vel[pl.ds(128 * c + 8 * i, 8), :] for c in range(3)] for i in range(16)}
    steps, own = [], []
    for k in (2, 13, 3, 12, 4, 11, 5, 10, 6, 9, 7, 8):
        step = net.eliminate(k)
        steps.append(step)
        own.append(forward(step, source))
    ends = (0, 1, 14, 15)
    out = [net.edge[e] for e in ((0, 1), (0, 14), (0, 15), (1, 14), (1, 15), (14, 15))]
    out += [net.ground[a] for a in ends] + [nu[a] for a in ends]
    out += [source[a][c] for a in ends for c in range(3)]
    for j, value in enumerate(out):
        xmsg[pl.ds(j, 8, stride=32), :] = value

    pl.semaphore_wait(barrier, 8 + 4 * core)

    @pl.when(core == 1)
    def pass_on():
        tell(near, "gy", place(0, 1))
        tell(near, "gy", place(0, -1))

    for k in (4, 3, 5, 2, 6, 1, 7):
        peer = lax.rem(chip + k, 8)
        push(0, xmsg, peer * 32, xin, gx * 32, 26, gx=peer * 2 + 1)

    @pl.when(core == 0)
    def lend():
        push(0, xmsg, chip * 32, xin, gx * 32, 26, gx=gx + 1)

    @pl.when(core == 1)
    def keep():
        xin[pl.ds(pl.multiple_of(gx * 32, 8), 26), :] = xmsg[
            pl.ds(pl.multiple_of(chip * 32, 8), 26), :
        ]

    eta = [visc[pl.ds(j, 16, stride=8), :] for j in range(8)]
    net = Network()
    for j in range(8):
        net.add_ground(j, 1.0)
        if j < 7:
            net.join(j, j + 1, eta[j] + eta[j + 1])
    net.add_ground(0, eta[0] * (gy == 0).astype(F32))
    net.add_ground(7, eta[7] * (gy == 15).astype(F32))
    ysteps = [net.eliminate(k) for k in (1, 6, 2, 5, 3, 4)]
    for j, value in enumerate((net.edge[(0, 7)], net.ground[0], net.ground[7], eta[0], eta[7])):
        by_row(cmsg, j, 5, value)

    xbase, xunit = responses(steps, own, ends)
    unused, yunit = responses(ysteps, [None] * 6, (0, 7))

    @pl.when(core == 1)
    def solve_ring():
        pl.semaphore_wait(near, 2)
        tell(far, "gy", place(0, 2))
        tell(far, "gy", place(0, -2))

        arrived(0, xin, 15 * 26)
        got = [xin[pl.ds(j, 16, stride=32), :] for j in range(26)]
        ring = Network()
        names = ("a", "b", "c", "d")
        for e, (i, j) in enumerate(((0, 1), (0, 2), (0, 3), (1, 2), (1, 3), (2, 3))):
            ring.join(names[i], names[j], got[e])
        for i in range(4):
            ring.add_ground(names[i], got[6 + i])
        rhs = {names[i]: got[14 + 3 * i : 17 + 3 * i] for i in range(4)}
        nu0, nu1, nu14, nu15 = got[10:14]

        def after(x, h):
            return pltpu.roll(x, 16 - h, 0)

        def before(x, h):
            return pltpu.roll(x, h, 0)

        last14, last15 = before(nu14, 1), before(nu15, 1)
        ring.join("a", "q", (last15 + nu0) * 0.5)
        ring.join("a", "p", (last14 + nu0) * 0.125)
        ring.join("b", "q", (last15 + nu1) * 0.125)
        rsteps = [ring.eliminate("a")]
        rown = [forward(rsteps[0], rhs)]
        rsteps.append(ring.eliminate("b"))
        rown.append(forward(rsteps[1], rhs))
        behind = [[ring.edge[("c", "p")], ring.edge[("c", "q")]], [ring.edge[("d", "p")], ring.edge[("d", "q")]]]
        onward = [[after(behind[j][i], 1) for j in range(2)] for i in range(2)]
        ground = [ring.ground["c"] + after(ring.ground["p"], 1), ring.ground["d"] + after(ring.ground["q"], 1)]
        inner = ring.edge[("c", "d")] + after(ring.edge[("p", "q")], 1)
        field = [
            [rhs[n][c] + after(rhs[m][c], 1) for c in range(3)] for n, m in (("c", "p"), ("d", "q"))
        ]

        def block_inverse(rest, link):
            scale = 1.0 / (rest[0] * rest[1] + link * (rest[0] + rest[1]))
            cross = link * scale
            return [[rest[1] * scale + cross, cross], [cross, rest[0] * scale + cross]]

        def times(m, v):
            return [[m[i][0] * v[0][j] + m[i][1] * v[1][j] for j in range(len(v[0]))] for i in range(2)]

        for h in (1, 2, 4):
            rest = [
                ground[i] + ((behind[i][0] + behind[i][1]) + (onward[i][0] + onward[i][1]))
                for i in range(2)
            ]
            inv = block_inverse(rest, inner)
            solved = times(inv, [[ground[i]] + field[i] + behind[i] + onward[i] for i in range(2)])
            up = [[after(x, h) for x in line] for line in solved]
            down = [[before(x, h) for x in line] for line in solved]
            from_up, from_down = times(onward, up), times(behind, down)
            ground = [ground[i] + from_up[i][0] + from_down[i][0] for i in range(2)]
            field = [
                [field[i][c] + from_up[i][1 + c] + from_down[i][1 + c] for c in range(3)]
                for i in range(2)
            ]
            inner = inner + from_up[0][5] + from_down[0][7]
            onward = [from_up[i][6:8] for i in range(2)]
            behind = [from_down[i][4:6] for i in range(2)]
        across = [[behind[i][j] + onward[i][j] for j in range(2)] for i in range(2)]
        rest = [ground[i] + (across[i][0] + across[i][1]) for i in range(2)]
        inv = block_inverse(rest, inner)
        solved = times(inv, [[ground[i]] + field[i] + [across[i][1]] for i in range(2)])
        other = times(across, [[after(x, 8) for x in line] for line in solved])
        ground = [ground[i] + other[i][0] for i in range(2)]
        field = [[field[i][c] + other[i][1 + c] for c in range(3)] for i in range(2)]
        inner = inner + other[0][4]
        value_c, value_d = times(block_inverse(ground, inner), field)
        value = {"c": value_c, "d": value_d}
        value["p"] = [before(x, 1) for x in value_c]
        value["q"] = [before(x, 1) for x in value_d]
        for (k, unused, ratio), y in zip(rsteps[::-1], rown[::-1]):
            value[k] = [summed([y[c]] + [r * value[a][c] for a, r in ratio.items()]) for c in range(3)]
        out = [value[n][c] for n in names for c in range(3)]
        for j, line in enumerate(out):
            xret[pl.ds(j, 16, stride=16), :] = line
        for k in (11, 3, 13, 5, 9, 7, 15, 12, 4, 8, 10, 14, 6, 2, 1):
            peer = lax.rem(gx + k, 16)
            push(2, xret, peer * 16, xback, chip * 16, 12, gx=peer)
        xback[pl.ds(pl.multiple_of(chip * 16, 8), 12), :] = xret[
            pl.ds(pl.multiple_of(gx * 16, 8), 12), :
        ]
        pl.semaphore_wait(far, 2)
        tell(go, "gx", gx - 1)

    @pl.when(core == 0)
    def follow():
        pl.semaphore_wait(go, 1)

    hand_in(1, cmsg, cin, 10)

    @pl.when(core == 1)
    def seven():
        arrived(2, xback, 7 * 12)

    @pl.when(core == 0)
    def eight():
        arrived(2, xback, 8 * 12)

    got = [xback[pl.ds(j, 8, stride=16), :] for j in range(12)]
    value = {a: got[3 * i : 3 * i + 3] for i, a in enumerate(ends)}
    for i in range(16):
        for c in range(3):
            if i in ends:
                x = value[i][c]
            else:
                x = summed([xbase[i][c]] + [w * value[a][c] for a, w in xunit[i].items()])
            half[pl.ds(128 * c + 8 * i, 8), :] = x

    lines = [[half[pl.ds(128 * c + j, 16, stride=8), :] for c in range(3)] for j in range(8)]
    for i, end in enumerate((0, 7)):
        for c in range(3):
            value = summed(
                [lines[end][c]] + [yunit[k][end] * lines[k][c] for k in range(1, 7) if end in yunit[k]]
            )
            by_row(ymsg, 3 * i + c, 6, value)
    hand_in(3, ymsg, yin, 12)
    source = {j: list(lines[j]) for j in range(8)}
    yown = [forward(step, source) for step in ysteps]
    ybase, unused = responses(ysteps, yown, (0, 7))

    segment = lax.broadcasted_iota(jnp.int32, (16, 128), 0)

    def lower(x, h):
        return pltpu.roll(x, h, 0)

    def upper(x, h):
        return pltpu.roll(x, 16 - h, 0)

    def factor(r):
        link, ground_a, ground_b, eta0, eta7 = [
            cin[pl.ds(5 * r + j, 16, stride=16), :] for j in range(5)
        ]
        gate = jnp.where(segment == 0, 0.0, lower(eta7, 1) + eta0)
        inverse_a = 1.0 / (ground_a + link + gate)
        to_b, to_q = link * inverse_a, gate * inverse_a
        low = to_q * link
        high = jnp.where(segment == 15, 0.0, upper(low, 1))
        to_b_up = jnp.where(segment == 15, 0.0, upper(to_q, 1))
        ground = ground_b + to_b * ground_a + to_b_up * upper(ground_a, 1)
        sweeps = []
        for h in (1, 2, 4, 8):
            inverse = 1.0 / (ground + low + high)
            weight_low, weight_high = low * lower(inverse, h), high * upper(inverse, h)
            sweeps.append((h, weight_low, weight_high))
            ground = ground + weight_low * lower(ground, h) + weight_high * upper(ground, h)
            low, high = weight_low * lower(low, h), weight_high * upper(high, h)
        return inverse_a, to_b, to_q, to_b_up, sweeps, 1.0 / ground

    def solve_row(r, factors):
        inverse_a, to_b, to_q, to_b_up, sweeps, inverse_b = factors
        for c in range(3):
            end_a = yin[pl.ds(6 * r + c, 16, stride=16), :]
            f = yin[pl.ds(6 * r + 3 + c, 16, stride=16), :]
            f = f + to_b * end_a + to_b_up * upper(end_a, 1)
            for h, weight_low, weight_high in sweeps:
                f = f + weight_low * lower(f, h) + weight_high * upper(f, h)
            f = f * inverse_b
            yret[pl.ds(6 * r + 3 + c, 16, stride=16), :] = f
            yret[pl.ds(6 * r + c, 16, stride=16), :] = (
                inverse_a * end_a + to_b * f + to_q * lower(f, 1)
            )

    def arrived_or(index, target, rows, count):
        @pl.when(own_rows == 1)
        def but_own():
            arrived(index, target, (count - 1) * rows)

        @pl.when(own_rows == 0)
        def with_all():
            arrived(index, target, count * rows)

    @pl.when(core == 1)
    def solve_rows():
        arrived_or(1, cin, 10, 16)
        factors = [factor(r) for r in range(2)]
        arrived_or(3, yin, 12, 16)
        for r in range(2):
            solve_row(r, factors[r])
        hand_back(4, yret, yback, 12)
        arrived_or(4, yback, 12, 8)

    @pl.when(core == 0)
    def await_rows():
        arrived(4, yback, 8 * 12)

    first = [by_row(yback, c, 6) for c in range(3)]
    final = [by_row(yback, 3 + c, 6) for c in range(3)]
    for c in range(3):
        for j in range(8):
            if j == 0:
                x = first[c]
            elif j == 7:
                x = final[c]
            else:
                x = ybase[j][c] + (yunit[j][0] * first[c] + yunit[j][7] * final[c])
            adv[pl.ds(128 * c + j, 16, stride=8), :] = x

    departed(0, xmsg, 7 * 26)
    departed(1, cmsg, 7 * 10)
    departed(3, ymsg, 7 * 12)

    @pl.when(core == 0)
    def lent():
        departed(0, xmsg, 26)
        departed(1, cmsg, 10)
        departed(3, ymsg, 12)

    @pl.when(core == 1)
    def returned():
        departed(2, xret, 15 * 12)
        departed(4, yret, 15 * 12)

        @pl.when(own_rows == 0)
        def all_returned():
            departed(1, cmsg, 10)
            departed(3, ymsg, 12)
            departed(4, yret, 12)


def store(half, adv, half_hbm, adv_hbm, done):
    copies = [
        pltpu.make_async_copy(half, half_hbm, done.at[0]),
        pltpu.make_async_copy(adv, adv_hbm, done.at[1]),
    ]
    for copy in copies:
        copy.start()
    for copy in copies:
        copy.wait()


def on_device(velocity, viscosity):
    vmem, hbm = pl.BlockSpec(memory_space=pltpu.VMEM), pl.BlockSpec(memory_space=pltpu.HBM)
    small, large = pltpu.VMEM((128, 128), F32), pltpu.VMEM((256, 128), F32)
    huge = pltpu.VMEM((512, 128), F32)
    held = [
        pltpu.with_memory_space_constraint(x, pltpu.HBM)
        for x in (velocity.reshape(384, 128), viscosity.reshape(128, 128))
    ]
    half, adv = pl.pallas_call(
        kernel,
        name="adi",
        out_shape=[jax.ShapeDtypeStruct((384, 128), F32)] * 2,
        in_specs=[hbm, hbm],
        out_specs=[vmem, vmem],
        scratch_shapes=[pltpu.VMEM((384, 128), F32), small, pltpu.SemaphoreType.DMA((2,)), large, huge, large, small, small, large, small, large, large, small]
        + [pltpu.SemaphoreType.DMA((5,)), pltpu.SemaphoreType.DMA((5,))]
        + [pltpu.SemaphoreType.REGULAR] * 3,
        compiler_params=pltpu.CompilerParams(
            collective_id=0, has_side_effects=True, vmem_limit_bytes=32 * 1024 * 1024
        ),
    )(*held)
    half, adv = pl.pallas_call(
        store,
        name="store",
        out_shape=[jax.ShapeDtypeStruct((384, 128), F32)] * 2,
        in_specs=[vmem, vmem],
        out_specs=[hbm, hbm],
        scratch_shapes=[pltpu.SemaphoreType.DMA((2,))],
        compiler_params=pltpu.CompilerParams(vmem_limit_bytes=1024 * 1024),
    )(half, adv)
    return half.reshape(velocity.shape), adv.reshape(velocity.shape)


def solution(mesh):
    return jax.shard_map(
        on_device,
        mesh=mesh,
        in_specs=(P(None, "gx", "gy", None), P("gx", "gy", None)),
        out_specs=(P(None, "gx", "gy", None), P(None, "gx", "gy", None)),
        check_vma=False,
    )
```

```python
import jax
import jax.numpy as jnp
from jax import lax
from jax.experimental import pallas as pl
from jax.experimental.pallas import tpu as pltpu
from jax.sharding import PartitionSpec as P

MESH = pl.DeviceIdType.MESH
F32 = jnp.float32
ORDER = (0, 4, 3, 7, 1, 5, 2, 6)
BACK = (0, 8, 1, 9, 2, 10, 3, 11, 7, 15, 6, 14, 5, 13, 4, 12)


class Network:
    def __init__(self):
        self.edge = {}
        self.ground = {}

    def join(self, a, b, w):
        k = (a, b) if a < b else (b, a)
        self.edge[k] = self.edge[k] + w if k in self.edge else w

    def add_ground(self, a, w):
        self.ground[a] = self.ground[a] + w if a in self.ground else w

    def eliminate(self, k):
        near = {}
        for a, b in list(self.edge):
            if k in (a, b):
                near[b if a == k else a] = self.edge.pop((a, b))
        ground = self.ground.pop(k)
        total = ground
        for w in near.values():
            total = total + w
        inverse = 1.0 / total
        ratio = {a: w * inverse for a, w in near.items()}
        names = sorted(near)
        for i, a in enumerate(names):
            self.add_ground(a, ratio[a] * ground)
            for b in names[i + 1 :]:
                self.join(a, b, ratio[a] * near[b])
        return k, inverse, ratio


def forward(step, source):
    k, inverse, ratio = step
    here = source.pop(k)
    for a, r in ratio.items():
        part = [r * h for h in here]
        source[a] = [s + t for s, t in zip(source[a], part)] if a in source else part
    return [h * inverse for h in here]


def summed(values):
    values = list(values)
    while len(values) > 1:
        values = [
            values[i] + values[i + 1] if i + 1 < len(values) else values[i]
            for i in range(0, len(values), 2)
        ]
    return values[0]


def responses(steps, own, terminals):
    base, unit = {}, {}
    for (k, inverse, ratio), y in reversed(list(zip(steps, own))):
        inner = [(a, r) for a, r in ratio.items() if a not in terminals]
        if y is not None:
            base[k] = [
                summed([y[c]] + [r * base[a][c] for a, r in inner]) for c in range(len(y))
            ]
        unit[k] = {}
        for t in terminals:
            terms = [r * unit[a][t] for a, r in inner if t in unit[a]]
            if t in ratio:
                terms.append(ratio[t])
            if terms:
                unit[k][t] = summed(terms)
    return base, unit


def kernel(
    vel_hbm, visc_hbm, half, adv,
    vel, visc, load, xmsg, xin, xret, xback, cmsg, cin, ymsg, yin, yret, yback, send, recv, near, far, go,
):
    gx, gy = lax.axis_index("gx"), lax.axis_index("gy")
    barrier = pltpu.get_barrier_semaphore()
    def place(side, move):
        return lax.rem(gy // 8 + side, 2) * 8 + lax.rem(gy + 8 + move, 8)

    def tell(semaphore, axis, peer):
        pl.semaphore_signal(semaphore, inc=1, device_id={axis: peer}, device_id_type=MESH)

    chip, core = gx // 2, lax.rem(gx, 2)

    around = (place(1, 1), place(1, -1), place(1, 0), place(0, 1), place(0, -1))

    @pl.when(core == 1)
    def announce():
        for peer in around:
            tell(barrier, "gy", peer)
        for k in (12, 4, 13, 11, 5, 3, 14, 10, 6, 2, 9, 7, 8, 1, 15):
            tell(barrier, "gx", lax.rem(gx + k, 16))

    loads = [
        pltpu.make_async_copy(visc_hbm, visc, load.at[0]),
        pltpu.make_async_copy(vel_hbm, vel, load.at[1]),
    ]
    for copy in loads:
        copy.start()

    def push(index, source, start, target, to, rows, **place):
        pltpu.make_async_remote_copy(
            src_ref=source.at[pl.ds(start if isinstance(start, int) else pl.multiple_of(start, 8), rows)],
            dst_ref=target.at[pl.ds(pl.multiple_of(to, 8), rows)],
            send_sem=send.at[index],
            recv_sem=recv.at[index],
            device_id=place,
            device_id_type=MESH,
        ).start()

    spot = lax.rem(gy, 8)
    swap = (chip == 0).astype(jnp.int32)
    upper_first, upper_second = swap, 1 - swap
    own_rows = (spot // 4 == upper_second).astype(jnp.int32)
    rank = (gy // 8) * 4 + lax.rem(spot, 4)

    def solver(at, upper):
        return (at // 4) * 8 + at % 4 + 4 * upper

    def stay(source, start, target, to, rows):
        target[pl.ds(pl.multiple_of(to, 8), rows), :] = source[
            pl.ds(pl.multiple_of(start, 8), rows), :
        ]

    def hand_in(index, source, target, rows):
        @pl.when(core == 0)
        def lend_rows():
            for at in ORDER:
                push(index, source, 16 * at, target, gy * 16, rows, gx=gx + 1, gy=solver(at, upper_first))

        @pl.when(core == 1)
        def give_rows():
            for at in ORDER:

                @pl.when(gy != solver(at, upper_second))
                def give_row(at=at):
                    push(index, source, 16 * at, target, gy * 16, rows, gx=gx, gy=solver(at, upper_second))

            @pl.when(own_rows == 1)
            def keep_row():
                stay(source, rank * 16, target, gy * 16, rows)

    def hand_back(index, source, target, rows):
        @pl.when(own_rows == 0)
        def return_rows():
            for at in BACK:
                push(index, source, 16 * at, target, rank * 16, rows, gx=gx - 1, gy=at)

        @pl.when(own_rows == 1)
        def pass_rows():
            for at in BACK:

                @pl.when(gy != at)
                def pass_row(at=at):
                    push(index, source, 16 * at, target, rank * 16, rows, gx=gx, gy=at)

            stay(source, gy * 16, target, rank * 16, rows)

    def by_row(ref, name, rows, value=None):
        if value is None:
            return jnp.concatenate(
                [ref[pl.ds(rows * r + name, 8, stride=16), :] for r in range(2)], axis=0
            )
        for r in range(2):
            ref[pl.ds(rows * r + name, 8, stride=16), :] = value[8 * r : 8 * r + 8]

    def arrived(index, target, rows):
        some = target.at[pl.ds(0, rows)]
        pltpu.make_async_copy(some, some, recv.at[index]).wait()

    def departed(index, source, rows):
        some = source.at[pl.ds(0, rows)]
        pltpu.make_async_copy(some, some, send.at[index]).wait()

    for copy in loads:
        copy.wait()

    nu = [visc[pl.ds(8 * i, 8), :] for i in range(16)]
    net = Network()
    for i in range(16):
        net.add_ground(i, 1.0)
        if i < 15:
            net.join(i, i + 1, (nu[i] + nu[i + 1]) * 0.5)
        if i < 14:
            net.join(i, i + 2, (nu[i] + nu[i + 2]) * 0.125)
    source = {i: [vel[pl.ds(128 * c + 8 * i, 8), :] for c in range(3)] for i in range(16)}
    steps, own = [], []
    for k in (2, 13, 3, 12, 4, 11, 5, 10, 6, 9, 7, 8):
        step = net.eliminate(k)
        steps.append(step)
        own.append(forward(step, source))
    ends = (0, 1, 14, 15)
    out = [net.edge[e] for e in ((0, 1), (0, 14), (0, 15), (1, 14), (1, 15), (14, 15))]
    out += [net.ground[a] for a in ends] + [nu[a] for a in ends]
    out += [source[a][c] for a in ends for c in range(3)]
    for j, value in enumerate(out):
        xmsg[pl.ds(j, 8, stride=32), :] = value

    pl.semaphore_wait(barrier, 8 + 4 * core)

    @pl.when(core == 1)
    def pass_on():
        tell(near, "gy", place(0, 1))
        tell(near, "gy", place(0, -1))

    for k in (4, 3, 5, 2, 6, 1, 7):
        peer = lax.rem(chip + k, 8)
        push(0, xmsg, peer * 32, xin, gx * 32, 26, gx=peer * 2 + 1)

    @pl.when(core == 0)
    def lend():
        push(0, xmsg, chip * 32, xin, gx * 32, 26, gx=gx + 1)

    @pl.when(core == 1)
    def keep():
        xin[pl.ds(pl.multiple_of(gx * 32, 8), 26), :] = xmsg[
            pl.ds(pl.multiple_of(chip * 32, 8), 26), :
        ]

    eta = [visc[pl.ds(j, 16, stride=8), :] for j in range(8)]
    net = Network()
    for j in range(8):
        net.add_ground(j, 1.0)
        if j < 7:
            net.join(j, j + 1, eta[j] + eta[j + 1])
    net.add_ground(0, eta[0] * (gy == 0).astype(F32))
    net.add_ground(7, eta[7] * (gy == 15).astype(F32))
    ysteps = [net.eliminate(k) for k in (1, 6, 2, 5, 3, 4)]
    for j, value in enumerate((net.edge[(0, 7)], net.ground[0], net.ground[7], eta[0], eta[7])):
        by_row(cmsg, j, 5, value)

    xbase, xunit = responses(steps, own, ends)
    unused, yunit = responses(ysteps, [None] * 6, (0, 7))

    @pl.when(core == 1)
    def solve_ring():
        pl.semaphore_wait(near, 2)
        tell(far, "gy", place(0, 2))
        tell(far, "gy", place(0, -2))

        arrived(0, xin, 15 * 26)
        names = (("a", "b", "c", "d"), ("e", "f", "g", "h"))
        ring, rhs, nu = Network(), {}, []
        for odd in range(2):
            name = names[odd]
            got = [xin[pl.ds(32 * odd + j, 8, stride=64), :] for j in range(26)]
            for e, (i, j) in enumerate(((0, 1), (0, 2), (0, 3), (1, 2), (1, 3), (2, 3))):
                ring.join(name[i], name[j], got[e])
            for i in range(4):
                ring.add_ground(name[i], got[6 + i])
                rhs[name[i]] = got[14 + 3 * i : 17 + 3 * i]
            nu.append(got[10:14])

        def after(x, h):
            return pltpu.roll(x, 8 - h, 0)

        def before(x, h):
            return pltpu.roll(x, h, 0)

        def bridge(left, right, c, d, a, b):
            ring.join(d, a, (left[3] + right[0]) * 0.5)
            ring.join(c, a, (left[2] + right[0]) * 0.125)
            ring.join(d, b, (left[3] + right[1]) * 0.125)

        bridge(nu[0], nu[1], "c", "d", "e", "f")
        bridge([before(x, 1) for x in nu[1]], nu[0], "p", "q", "a", "b")
        rsteps, rown = [], []
        for k in "afbecd":
            rsteps.append(ring.eliminate(k))
            rown.append(forward(rsteps[-1], rhs))
        behind = [[ring.edge[("g", "p")], ring.edge[("g", "q")]], [ring.edge[("h", "p")], ring.edge[("h", "q")]]]
        onward = [[after(behind[j][i], 1) for j in range(2)] for i in range(2)]
        ground = [ring.ground["g"] + after(ring.ground["p"], 1), ring.ground["h"] + after(ring.ground["q"], 1)]
        inner = ring.edge[("g", "h")] + after(ring.edge[("p", "q")], 1)
        field = [
            [rhs[n][c] + after(rhs[m][c], 1) for c in range(3)] for n, m in (("g", "p"), ("h", "q"))
        ]

        def block_inverse(rest, link):
            scale = 1.0 / (rest[0] * rest[1] + link * (rest[0] + rest[1]))
            cross = link * scale
            return [[rest[1] * scale + cross, cross], [cross, rest[0] * scale + cross]]

        def times(m, v):
            return [[m[i][0] * v[0][j] + m[i][1] * v[1][j] for j in range(len(v[0]))] for i in range(2)]

        for h in (1, 2):
            rest = [
                ground[i] + ((behind[i][0] + behind[i][1]) + (onward[i][0] + onward[i][1]))
                for i in range(2)
            ]
            inv = block_inverse(rest, inner)
            solved = times(inv, [[ground[i]] + field[i] + behind[i] + onward[i] for i in range(2)])
            up = [[after(x, h) for x in line] for line in solved]
            down = [[before(x, h) for x in line] for line in solved]
            from_up, from_down = times(onward, up), times(behind, down)
            ground = [ground[i] + from_up[i][0] + from_down[i][0] for i in range(2)]
            field = [
                [field[i][c] + from_up[i][1 + c] + from_down[i][1 + c] for c in range(3)]
                for i in range(2)
            ]
            inner = inner + from_up[0][5] + from_down[0][7]
            onward = [from_up[i][6:8] for i in range(2)]
            behind = [from_down[i][4:6] for i in range(2)]
        across = [[behind[i][j] + onward[i][j] for j in range(2)] for i in range(2)]
        rest = [ground[i] + (across[i][0] + across[i][1]) for i in range(2)]
        inv = block_inverse(rest, inner)
        solved = times(inv, [[ground[i]] + field[i] + [across[i][1]] for i in range(2)])
        other = times(across, [[after(x, 4) for x in line] for line in solved])
        ground = [ground[i] + other[i][0] for i in range(2)]
        field = [[field[i][c] + other[i][1 + c] for c in range(3)] for i in range(2)]
        inner = inner + other[0][4]
        value_g, value_h = times(block_inverse(ground, inner), field)
        value = {"g": value_g, "h": value_h}
        value["p"] = [before(x, 1) for x in value_g]
        value["q"] = [before(x, 1) for x in value_h]
        for (k, unused, ratio), y in zip(rsteps[::-1], rown[::-1]):
            value[k] = [summed([y[c]] + [r * value[a][c] for a, r in ratio.items()]) for c in range(3)]
        for odd in range(2):
            for i, name in enumerate(names[odd]):
                for c in range(3):
                    xret[pl.ds(16 * odd + 3 * i + c, 8, stride=32), :] = value[name][c]
        for k in (11, 3, 13, 5, 9, 7, 15, 12, 4, 8, 10, 14, 6, 2, 1):
            peer = lax.rem(gx + k, 16)
            push(2, xret, peer * 16, xback, chip * 16, 12, gx=peer)
        xback[pl.ds(pl.multiple_of(chip * 16, 8), 12), :] = xret[
            pl.ds(pl.multiple_of(gx * 16, 8), 12), :
        ]
        pl.semaphore_wait(far, 2)
        tell(go, "gx", gx - 1)

    @pl.when(core == 0)
    def follow():
        pl.semaphore_wait(go, 1)

    hand_in(1, cmsg, cin, 10)

    @pl.when(core == 1)
    def seven():
        arrived(2, xback, 7 * 12)

    @pl.when(core == 0)
    def eight():
        arrived(2, xback, 8 * 12)

    got = [xback[pl.ds(j, 8, stride=16), :] for j in range(12)]
    value = {a: got[3 * i : 3 * i + 3] for i, a in enumerate(ends)}
    for i in range(16):
        for c in range(3):
            if i in ends:
                x = value[i][c]
            else:
                x = summed([xbase[i][c]] + [w * value[a][c] for a, w in xunit[i].items()])
            half[pl.ds(128 * c + 8 * i, 8), :] = x

    lines = [[half[pl.ds(128 * c + j, 16, stride=8), :] for c in range(3)] for j in range(8)]
    for i, end in enumerate((0, 7)):
        for c in range(3):
            value = summed(
                [lines[end][c]] + [yunit[k][end] * lines[k][c] for k in range(1, 7) if end in yunit[k]]
            )
            by_row(ymsg, 3 * i + c, 6, value)
    hand_in(3, ymsg, yin, 12)
    source = {j: list(lines[j]) for j in range(8)}
    yown = [forward(step, source) for step in ysteps]
    ybase, unused = responses(ysteps, yown, (0, 7))

    segment = lax.broadcasted_iota(jnp.int32, (16, 128), 0)

    def lower(x, h):
        return pltpu.roll(x, h, 0)

    def upper(x, h):
        return pltpu.roll(x, 16 - h, 0)

    def factor(r):
        link, ground_a, ground_b, eta0, eta7 = [
            cin[pl.ds(5 * r + j, 16, stride=16), :] for j in range(5)
        ]
        gate = jnp.where(segment == 0, 0.0, lower(eta7, 1) + eta0)
        inverse_a = 1.0 / (ground_a + link + gate)
        to_b, to_q = link * inverse_a, gate * inverse_a
        low = to_q * link
        high = jnp.where(segment == 15, 0.0, upper(low, 1))
        to_b_up = jnp.where(segment == 15, 0.0, upper(to_q, 1))
        ground = ground_b + to_b * ground_a + to_b_up * upper(ground_a, 1)
        sweeps = []
        for h in (1, 2, 4, 8):
            inverse = 1.0 / (ground + low + high)
            weight_low, weight_high = low * lower(inverse, h), high * upper(inverse, h)
            sweeps.append((h, weight_low, weight_high))
            ground = ground + weight_low * lower(ground, h) + weight_high * upper(ground, h)
            low, high = weight_low * lower(low, h), weight_high * upper(high, h)
        return inverse_a, to_b, to_q, to_b_up, sweeps, 1.0 / ground

    def solve_row(r, factors):
        inverse_a, to_b, to_q, to_b_up, sweeps, inverse_b = factors
        for c in range(3):
            end_a = yin[pl.ds(6 * r + c, 16, stride=16), :]
            f = yin[pl.ds(6 * r + 3 + c, 16, stride=16), :]
            f = f + to_b * end_a + to_b_up * upper(end_a, 1)
            for h, weight_low, weight_high in sweeps:
                f = f + weight_low * lower(f, h) + weight_high * upper(f, h)
            f = f * inverse_b
            yret[pl.ds(6 * r + 3 + c, 16, stride=16), :] = f
            yret[pl.ds(6 * r + c, 16, stride=16), :] = (
                inverse_a * end_a + to_b * f + to_q * lower(f, 1)
            )

    def arrived_or(index, target, rows, count):
        @pl.when(own_rows == 1)
        def but_own():
            arrived(index, target, (count - 1) * rows)

        @pl.when(own_rows == 0)
        def with_all():
            arrived(index, target, count * rows)

    @pl.when(core == 1)
    def solve_rows():
        arrived_or(1, cin, 10, 16)
        factors = [factor(r) for r in range(2)]
        arrived_or(3, yin, 12, 16)
        for r in range(2):
            solve_row(r, factors[r])
        hand_back(4, yret, yback, 12)
        arrived_or(4, yback, 12, 8)

    @pl.when(core == 0)
    def await_rows():
        arrived(4, yback, 8 * 12)

    first = [by_row(yback, c, 6) for c in range(3)]
    final = [by_row(yback, 3 + c, 6) for c in range(3)]
    for c in range(3):
        for j in range(8):
            if j == 0:
                x = first[c]
            elif j == 7:
                x = final[c]
            else:
                x = ybase[j][c] + (yunit[j][0] * first[c] + yunit[j][7] * final[c])
            adv[pl.ds(128 * c + j, 16, stride=8), :] = x

    departed(0, xmsg, 7 * 26)
    departed(1, cmsg, 7 * 10)
    departed(3, ymsg, 7 * 12)

    @pl.when(core == 0)
    def lent():
        departed(0, xmsg, 26)
        departed(1, cmsg, 10)
        departed(3, ymsg, 12)

    @pl.when(core == 1)
    def returned():
        departed(2, xret, 15 * 12)
        departed(4, yret, 15 * 12)

        @pl.when(own_rows == 0)
        def all_returned():
            departed(1, cmsg, 10)
            departed(3, ymsg, 12)
            departed(4, yret, 12)


def store(half, adv, half_hbm, adv_hbm, done):
    copies = [
        pltpu.make_async_copy(half, half_hbm, done.at[0]),
        pltpu.make_async_copy(adv, adv_hbm, done.at[1]),
    ]
    for copy in copies:
        copy.start()
    for copy in copies:
        copy.wait()


def on_device(velocity, viscosity):
    vmem, hbm = pl.BlockSpec(memory_space=pltpu.VMEM), pl.BlockSpec(memory_space=pltpu.HBM)
    small, large = pltpu.VMEM((128, 128), F32), pltpu.VMEM((256, 128), F32)
    huge = pltpu.VMEM((512, 128), F32)
    held = [
        pltpu.with_memory_space_constraint(x, pltpu.HBM)
        for x in (velocity.reshape(384, 128), viscosity.reshape(128, 128))
    ]
    half, adv = pl.pallas_call(
        kernel,
        name="adi",
        out_shape=[jax.ShapeDtypeStruct((384, 128), F32)] * 2,
        in_specs=[hbm, hbm],
        out_specs=[vmem, vmem],
        scratch_shapes=[pltpu.VMEM((384, 128), F32), small, pltpu.SemaphoreType.DMA((2,)), large, huge, large, small, small, large, small, large, large, small]
        + [pltpu.SemaphoreType.DMA((5,)), pltpu.SemaphoreType.DMA((5,))]
        + [pltpu.SemaphoreType.REGULAR] * 3,
        compiler_params=pltpu.CompilerParams(
            collective_id=0, has_side_effects=True, vmem_limit_bytes=32 * 1024 * 1024
        ),
    )(*held)
    half, adv = pl.pallas_call(
        store,
        name="store",
        out_shape=[jax.ShapeDtypeStruct((384, 128), F32)] * 2,
        in_specs=[vmem, vmem],
        out_specs=[hbm, hbm],
        scratch_shapes=[pltpu.SemaphoreType.DMA((2,))],
        compiler_params=pltpu.CompilerParams(vmem_limit_bytes=1024 * 1024),
    )(half, adv)
    return half.reshape(velocity.shape), adv.reshape(velocity.shape)


def solution(mesh):
    return jax.shard_map(
        on_device,
        mesh=mesh,
        in_specs=(P(None, "gx", "gy", None), P("gx", "gy", None)),
        out_specs=(P(None, "gx", "gy", None), P(None, "gx", "gy", None)),
        check_vma=False,
    )
```
